128 devices in a mesh: section: 8 (over y, core), dp: 16 (over x, z).
Axes of the slice: x: 4, y: 4, z: 4, core: 2. Of those that a mesh axis runs over, the one named last changes fastest.
Arguments:
- old_slot: int32 [24], replicated, may hold values from 0 to 23, as said below
- new_slot: int32 [24], replicated, may hold values from 0 to 23, as said below
- a_old: bfloat16 [24, 64, 16384], P('section', None, 'dp'), may hold values from -0.046875 to 0.046875
- a_first_old: float32 [24, 64, 16384], P('section', None, 'dp'), may hold values from -3 to 3
- a_second_old: float32 [24, 64, 16384], P('section', None, 'dp'), may hold values from 0.01 to 1
- b_old: bfloat16 [24, 64, 1024], P('section', None, 'dp'), may hold values from -0.75 to 0.75
- b_first_old: float32 [24, 64, 1024], P('section', None, 'dp'), may hold values from -0.75 to 0.75
- b_second_old: float32 [24, 64, 1024], P('section', None, 'dp'), may hold values from 0.005 to 0.5
- inputs: bfloat16 [16, 4096, 16384], P('section', 'dp'), may hold values from -6 to 6
- cotangent: bfloat16 [16, 4096, 1024], P('section', 'dp'), may hold values from -0.005859375 to 0.005859375
Outputs:
- adapter_out: bfloat16 [16, 4096, 1024], P('section', 'dp')
- new_a: bfloat16 [32, 64, 16384], P('section', None, 'dp')
- new_b: bfloat16 [32, 64, 1024], P('section', None, 'dp')
- a_first_new: float32 [32, 64, 16384], P('section', None, 'dp')
- a_second_new: float32 [32, 64, 16384], P('section', None, 'dp')
- b_first_new: float32 [32, 64, 1024], P('section', None, 'dp')
- b_second_new: float32 [32, 64, 1024], P('section', None, 'dp')
- a_step: float32 [16, 64, 16384], P('section', None, 'dp')
- b_step: float32 [16, 64, 1024], P('section', None, 'dp')
The draws below stay inside these ranges and needn't reach their ends.
Inputs may be any that keep to these rules, and one draw needn't show every extreme that they name: `old_slot`: A permutation of the old slots; old slot i lies on section i // 3, so every old slot holds a layer. `new_slot`: distinct values filling every slot of the first 6 sections (new slot i lies on section i // 4); the last sections hold no layer; no two layers that share an old section share a new section.
All inputs are finite; a program needn't handle non-finite values.
Results may differ from the reference program's by a relative error of at most 0.0049.
Values may be sent and summed in bfloat16 or wider, within the bound.
A program may use at most 128 MiB of HBM per device.

```python
import math
import jax
import jax.numpy as jnp
from jax import lax

D = 16384
KV = 1024
R = 64
OLD_DEV = 3
NEW_DEV = 4
WIN = 2
TOK_DEV = 256
LAYERS = 24
N_NEW = 6
TOKENS = 4096
N_SECTION = 8
N_DP = 16


def section_maps(key):
    keys = jax.random.split(key, 4)
    layer_order = jax.random.permutation(keys[0], LAYERS)
    section_rank = jax.random.permutation(keys[1], N_SECTION)
    target = jax.random.permutation(keys[2], N_NEW)
    scores = jax.random.randint(keys[3], (N_SECTION, OLD_DEV), 0, 1 << 20) * OLD_DEV + jnp.arange(OLD_DEV)[None, :]
    within = jnp.argsort(scores, axis=1, stable=True)
    slots = jnp.arange(LAYERS)
    section_of = slots // OLD_DEV
    place = slots % OLD_DEV
    order = section_rank[section_of] * OLD_DEV + within[section_of, place]
    new_of_old = target[order % N_NEW] * NEW_DEV + order // N_NEW
    return (layer_order.astype(jnp.int32), new_of_old[layer_order].astype(jnp.int32))


def draw_old_slot(key, part):
    return section_maps(key)[0]


def draw_new_slot(key, part):
    return section_maps(key)[1]


def with_spikes(array, key, source, target, parts, factor):
    def block_of(position):
        return (jnp.arange(array.shape[position]) // (array.shape[position] // parts)).reshape((-1,) + (1,) * (array.ndim - 1 - position))

    one_side = jax.random.permutation(key, parts)[block_of(target)]
    far = (block_of(target) + parts // 2) % parts
    return jnp.where((block_of(source) == one_side) | (block_of(source) == far), factor * array, array)


def block_levels(key, dims, pieces, low, high):
    loudness, own = 1.0, jax.random.fold_in(key, 6)
    for dim, blocks in pieces:
        steps = jnp.exp(jax.random.uniform(jax.random.fold_in(own, dim), (blocks,), jnp.float32, low / len(pieces), high / len(pieces)))
        loudness = loudness * jnp.repeat(steps, dims[dim] // blocks).reshape([-1 if axis == dim else 1 for axis in range(len(dims))])
    return loudness


def noise(stream_key, shape, width, bound, shards=(), kind=jnp.bfloat16):
    factor_of = block_levels(stream_key, shape, shards, -0.22, 0.18) if shards else 1.0
    drawn = jax.random.normal(stream_key, shape, jnp.float32) * width * factor_of
    return jnp.minimum(jnp.maximum(drawn, -bound), bound).astype(kind)


def gaussian_with(key, extent, scale, reach, pieces, heavy, held_as=jnp.bfloat16):
    values = scale * jax.random.normal(key, extent, jnp.float32)
    if pieces:
        values = values * block_levels(key, extent, pieces, -0.22, 0.18)
    return jnp.clip(with_spikes(values, jax.random.fold_in(key, 3), *heavy), -reach, reach).astype(held_as)


def setup_inputs(seed: int = 0) -> dict:
    key_list = jax.random.split(jax.random.key(seed), 11)
    old_slot = draw_old_slot(jax.random.fold_in(key_list[10], 71), 0)
    new_slot = draw_new_slot(jax.random.fold_in(key_list[10], 71), 0)
    a_old = noise(key_list[2], (LAYERS, R, D), D ** -0.5, 0.046875, ((0, 8), (2, 16)))
    a_first_old = noise(key_list[3], (LAYERS, R, D), 0.5, 3.0, ((0, 8), (2, 16)), jnp.float32)
    a_second_old = jnp.clip(jnp.exp(math.log(1.0) - 4.6051702 * jax.random.uniform(key_list[4], (LAYERS, R, D), jnp.float32) ** block_levels(key_list[4], (LAYERS, R, D), ((0, 8), (2, 16)), -0.2, 0.2)), 0.01, 1.0)
    b_old = noise(key_list[5], (LAYERS, R, KV), R ** -0.5, 0.75, ((0, 8), (2, 16)))
    b_first_old = noise(key_list[6], (LAYERS, R, KV), 0.125, 0.75, ((0, 8), (2, 16)), jnp.float32)
    b_second_old = jnp.clip(jnp.exp(math.log(0.5) - 4.6051702 * jax.random.uniform(key_list[7], (LAYERS, R, KV), jnp.float32) ** block_levels(key_list[7], (LAYERS, R, KV), ((0, 8), (2, 16)), -0.2, 0.2)), 0.005, 0.5)
    inputs = gaussian_with(key_list[8], (N_SECTION * WIN, TOKENS, D), 1.0, 6.0, ((0, 8), (1, 16)), (1, 2, 16, 2.0))
    cotangent = noise(key_list[9], (N_SECTION * WIN, TOKENS, KV), (0.25 * (R / (KV * TOK_DEV * N_DP)) ** 0.5), 0.005859375, ((0, 8), (1, 16)))
    return {"old_slot": old_slot, "new_slot": new_slot, "a_old": a_old, "a_first_old": a_first_old, "a_second_old": a_second_old, "b_old": b_old, "b_first_old": b_first_old, "b_second_old": b_second_old, "inputs": inputs, "cotangent": cotangent}


adapter_scale = 2.0
beta_one = 0.9
beta_two = 0.999
adam_eps = 1e-08
corr_one = 1.0 - (0.9 ** 10) ** 10
corr_two = 1.0 - (0.999 ** 10) ** 10

def relocate(old_state, old_slot, new_slot):
    fresh = jnp.zeros((N_SECTION * NEW_DEV,) + old_state.shape[1:], old_state.dtype)
    return fresh.at[new_slot].set(old_state[old_slot])

def adam_update(first, second, grad):
    first_new = beta_one * first + (1.0 - beta_one) * grad
    second_new = beta_two * second + (1.0 - beta_two) * grad * grad
    direction = first_new / corr_one / (jnp.sqrt(second_new / corr_two) + adam_eps)
    return (first_new, second_new, direction)

def window_layer(item):
    input_tokens, incoming_gradient, factor_a, up_factor_matrix = item
    low_rank_hidden = jnp.dot(input_tokens, factor_a.T, preferred_element_type=jnp.float32).astype(jnp.bfloat16)
    adapted_output = (adapter_scale * jnp.dot(low_rank_hidden, up_factor_matrix, preferred_element_type=jnp.float32)).astype(jnp.bfloat16)
    fetched_rows = jnp.dot(incoming_gradient, up_factor_matrix.T, preferred_element_type=jnp.float32).astype(jnp.bfloat16)
    down_factor_gradient = adapter_scale * jnp.dot(fetched_rows.T, input_tokens, preferred_element_type=jnp.float32)
    up_factor_gradient = adapter_scale * jnp.dot(low_rank_hidden.T, incoming_gradient, preferred_element_type=jnp.float32)
    return (adapted_output, down_factor_gradient, up_factor_gradient)

def reference(old_slot, new_slot, a_old, a_first_old, a_second_old, b_old, b_first_old, b_second_old, inputs, cotangent):
    new_a = relocate(a_old, old_slot, new_slot)
    new_b = relocate(b_old, old_slot, new_slot)
    a_first = relocate(a_first_old, old_slot, new_slot)
    a_second = relocate(a_second_old, old_slot, new_slot)
    b_first = relocate(b_first_old, old_slot, new_slot)
    b_second = relocate(b_second_old, old_slot, new_slot)
    window = (jnp.arange(N_SECTION, dtype=jnp.int32)[:, None] * NEW_DEV + jnp.arange(WIN, dtype=jnp.int32)[None, :]).reshape(-1)
    adapted_output, down_factor_gradient, up_factor_gradient = lax.map(window_layer, (inputs, cotangent, new_a[window], new_b[window]))
    first_a, second_a, step_a = adam_update(a_first[window], a_second[window], down_factor_gradient)
    first_b, second_b, step_b = adam_update(b_first[window], b_second[window], up_factor_gradient)
    a_first = a_first.at[window].set(first_a)
    a_second = a_second.at[window].set(second_a)
    b_first = b_first.at[window].set(first_b)
    b_second = b_second.at[window].set(second_b)
    return (adapted_output, new_a, new_b, a_first, a_second, b_first, b_second, step_a, step_b)
```

```python
import jax
import jax.numpy as jnp
from jax import lax
from jax.experimental import pallas as pl
from jax.experimental.pallas import tpu as pltpu
from jax.sharding import PartitionSpec as P

MESH = pl.DeviceIdType.MESH
F32 = jnp.float32
BF16 = jnp.bfloat16

OLD_DEV = 3
NEW_DEV = 4
WIN = 2
LAYERS = 24
N_SECTION = 8
N_NEW = 6
N_DP = 16
SIDE = 4
R = 64
HALF = 32
TOK = 256
LD = 1024
LK = 64
KV = 1024

adapter_scale = 2.0
beta_one = 0.9
beta_two = 0.999
adam_eps = 1e-08
corr_one = 1.0 - (0.9**10) ** 10
corr_two = 1.0 - (0.999**10) ** 10


def dot_nt(a, b):
    return lax.dot_general(a, b, (((1,), (1,)), ((), ())), preferred_element_type=F32)


def dot_nn(a, b):
    return jnp.dot(a, b, preferred_element_type=F32)


class Messages:
    def __init__(self, send_sem, recv_sem):
        self.send_sem, self.recv_sem = send_sem, recv_sem
        self.count = 0

    def make(self, src, dst, device):
        i = self.count
        self.count += 1
        return pltpu.make_async_remote_copy(
            src_ref=src,
            dst_ref=dst,
            send_sem=self.send_sem.at[i],
            recv_sem=self.recv_sem.at[i],
            device_id=device,
            device_id_type=MESH,
        )


N_MSG = 200


def exchange_kernel(
    old_slot,
    new_slot,
    a_old,
    a_first_old,
    a_second_old,
    b_old,
    b_first_old,
    b_second_old,
    inputs,
    cotangent,
    pa_out,
    pm_out,
    pb_out,
    pbm_out,
    ga_out,
    gb_out,
    lat_out,
    bw_out,
    xin,
    cot,
    av,
    mv1,
    mv2,
    bv,
    bmv1,
    bmv2,
    b_stage,
    b_recv,
    bm_stage,
    bm_recv,
    a_stage0,
    a_stage1,
    a_recv0,
    a_recv1,
    m_stage,
    m_recv,
    afull,
    bfull,
    bw,
    pulled,
    lat_acc,
    lat,
    gb_stage,
    gb_recv,
    gsend,
    grecv,
    hbuf,
    hsend,
    hrecv,
    pa,
    pm,
    pb,
    pbm,
    ga,
    gb,
    send_sem,
    recv_sem,
    load_sem,
    x_sem,
    out_sem,
):
    me_s = lax.axis_index("section")
    me_d = lax.axis_index("dp")
    mx = me_d // SIDE
    mz = me_d % SIDE

    def at(dx, dz):
        return ((mx + dx) % SIDE) * SIDE + (mz + dz) % SIDE

    msgs = Messages(send_sem, recv_sem)

    def load(src, dst, i):
        c = pltpu.make_async_copy(src, dst, load_sem.at[i])
        c.start()
        return c

    ld_b = load(b_old, bv, 0)
    ld_a = load(a_old, av, 1)

    barrier = pltpu.get_barrier_semaphore()
    for j in range(1, N_DP):
        pl.semaphore_signal(
            barrier, inc=1, device_id=(me_s, (me_d + j) % N_DP), device_id_type=MESH
        )
    for k in range(1, N_SECTION):
        pl.semaphore_signal(
            barrier, inc=1, device_id=((me_s + k) % N_SECTION, me_d), device_id_type=MESH
        )

    ld_cot = load(cotangent, cot, 2)
    ld_b1 = load(b_first_old, bmv1, 3)
    ld_b2 = load(b_second_old, bmv2, 4)

    def x_copy(w, a, b):
        ax = at(b, a) if w == 0 else at(a, b)
        return pltpu.make_async_copy(
            inputs.at[w, :, pl.ds(pl.multiple_of(ax * LD, LD), LD)],
            xin.at[w, a, b],
            x_sem.at[w, a, b],
        )

    dest = []
    for j in range(OLD_DEV):
        total = jnp.int32(0)
        for l in range(LAYERS):
            total += jnp.where(old_slot[l] == me_s * OLD_DEV + j, new_slot[l] // NEW_DEV, 0)
        dest.append(total)
    src_k, present = [], []
    for s in range(NEW_DEV):
        total, has = jnp.int32(0), jnp.int32(0)
        for l in range(LAYERS):
            hit = new_slot[l] == me_s * NEW_DEV + s
            total += jnp.where(hit, old_slot[l] // OLD_DEV, 0)
            has += jnp.where(hit, 1, 0)
        src_k.append((me_s + N_SECTION - total) % N_SECTION)
        present.append(has > 0)
    send_index = []
    for k in range(N_SECTION):
        d = (me_s + k) % N_SECTION
        pick = jnp.int32(0)
        for j in range(1, OLD_DEV):
            pick = jnp.where(dest[j] == d, j, pick)
        send_index.append(pick)

    receives = me_s < N_NEW

    def peer(k):
        return ((me_s + k) % N_SECTION, me_d)

    def sends_to(k):
        return (me_s + k) % N_SECTION < N_NEW

    def pack_b(v):
        v = v.astype(F32)
        return jnp.concatenate([v[:HALF], v[HALF:]], axis=1).astype(BF16)

    @pl.when(jnp.logical_not(receives))
    def _():
        b_recv[...] = jnp.zeros_like(b_recv)
        bm_recv[...] = jnp.zeros_like(bm_recv)
        a_recv0[...] = jnp.zeros_like(a_recv0)
        a_recv1[...] = jnp.zeros_like(a_recv1)
        m_recv[...] = jnp.zeros_like(m_recv)

    ld_b.wait()
    for k in range(N_SECTION):
        v = pack_b(bv[send_index[k]])
        if k == 0:
            b_recv[0] = v
        else:
            b_stage[k] = v
    b_msgs = {
        k: msgs.make(b_stage.at[k], b_recv.at[k], peer(k)) for k in range(1, N_SECTION)
    }
    pl.semaphore_wait(barrier, N_DP - 1 + N_SECTION - 1)

    def start_all(group):
        for k, m in group.items():
            @pl.when(sends_to(k))
            def _(m=m):
                m.start()

    def recv_all(group):
        @pl.when(receives)
        def _():
            for m in group.values():
                m.wait_recv()

    def wait_sent(group):
        for k, m in group.items():
            @pl.when(sends_to(k))
            def _(m=m):
                m.wait_send()

    start_all(b_msgs)

    ld_a.wait()
    a_stage, a_recv = (a_stage0, a_stage1), (a_recv0, a_recv1)
    a_msgs = []
    for h in range(2):
        for k in range(N_SECTION):
            v = av[send_index[k], pl.ds(h * HALF, HALF), :]
            if k == 0:
                a_recv[h][0] = v
            else:
                a_stage[h][k] = v
        group = {
            k: msgs.make(a_stage[h].at[k], a_recv[h].at[k], peer(k))
            for k in range(1, N_SECTION)
        }
        start_all(group)
        a_msgs.append(group)

    for w in range(WIN):
        for b in range(SIDE):
            for a in range(SIDE):
                x_copy(w, a, b).start()
    ld_m1 = load(a_first_old, mv1, 5)
    ld_m2 = load(a_second_old, mv2, 6)

    recv_all(b_msgs)

    def unpack_b(v):
        v = v.astype(F32)
        return jnp.concatenate([v[:, :LK], v[:, LK:]], axis=0)

    pbs = []
    for s in range(NEW_DEV):
        v = b_recv[src_k[s]]
        v = jnp.where(present[s], v, jnp.zeros_like(v))
        pb[s] = v
        if s < WIN:
            pbs.append(unpack_b(v))
    bfull[me_d] = jnp.concatenate(pbs, axis=1).astype(BF16)
    bg_msgs = []
    for j in range(1, N_DP):
        m = msgs.make(bfull.at[me_d], bfull.at[me_d], (me_s, (me_d + j) % N_DP))
        m.start()
        bg_msgs.append(m)

    def nbr(w, axis, step):
        on_x = (axis == 1) == (w == 0)
        return (me_s, at(step, 0) if on_x else at(0, step))

    ag = {}
    PLUS, MINUS = 1, 3

    def ag_make(w, a, b, h, axis, step):
        na, nb = (a, b)
        if axis == 0:
            na = (a - step) % SIDE
        else:
            nb = (b - step) % SIDE
        rows = pl.ds(h * HALF, HALF)
        m = msgs.make(
            afull.at[w, a, b, rows], afull.at[w, na, nb, rows], nbr(w, axis, step)
        )
        assert (w, na, nb, h) not in ag
        ag[(w, na, nb, h)] = m
        m.start()

    def ag_on(w, a, b, h):
        if b == 0:
            if a == 0:
                ag_make(w, a, b, h, 0, 1)
                ag_make(w, a, b, h, 0, -1)
            elif a == 3 and h == 0:
                ag_make(w, a, b, h, 0, 1)
            elif a == 1 and h == 1:
                ag_make(w, a, b, h, 0, -1)
            ag_make(w, a, b, h, 1, 1)
            ag_make(w, a, b, h, 1, -1)
        elif b == 3 and h == 0:
            ag_make(w, a, b, h, 1, 1)
        elif b == 1 and h == 1:
            ag_make(w, a, b, h, 1, -1)

    for h in range(2):
        recv_all(a_msgs[h])
        rows = pl.ds(h * HALF, HALF)
        for s in range(NEW_DEV):
            v = a_recv[h][src_k[s]]
            v = jnp.where(present[s], v, jnp.zeros_like(v))
            pa[s, rows] = v
            if s < WIN:
                afull[s, 0, 0, rows] = v
                ag_on(s, 0, 0, h)

    ld_b1.wait()
    ld_b2.wait()
    ld_m1.wait()
    ld_m2.wait()
    for k in range(N_SECTION):
        bm = jnp.concatenate([bmv1[send_index[k]], bmv2[send_index[k]]], axis=1).astype(BF16)
        for i, mv in enumerate((mv1, mv2)):
            v = mv[send_index[k]].astype(BF16)
            if k == 0:
                m_recv[0, i] = v
            else:
                m_stage[k, i] = v
        if k == 0:
            bm_recv[0] = bm
        else:
            bm_stage[k] = bm
    bm_msgs = {
        k: msgs.make(bm_stage.at[k], bm_recv.at[k], peer(k)) for k in range(1, N_SECTION)
    }
    m_msgs = {k: msgs.make(m_stage.at[k], m_recv.at[k], peer(k)) for k in range(1, N_SECTION)}
    start_all(bm_msgs)
    start_all(m_msgs)

    for j in range(1, N_DP):
        bg_msgs[j - 1].wait_recv()
    for d in range(0, N_DP, 2):
        lo, hi = bfull[d].astype(F32), bfull[d + 1].astype(F32)
        cols = pl.ds(d * LK, 2 * LK)
        bw[0, :, cols] = jnp.concatenate([lo[:, :LK], hi[:, :LK]], axis=1).astype(BF16)
        bw[1, :, cols] = jnp.concatenate([lo[:, LK:], hi[:, LK:]], axis=1).astype(BF16)
    ld_cot.wait()
    for w in range(WIN):
        pulled[w] = dot_nt(bw[w], cot[w]).astype(BF16)

    for w in range(WIN):
        for b in range(SIDE):
            for a in range(SIDE):
                x_copy(w, a, b).wait()

    def partial(w, f, s):
        return dot_nn(pulled[w], xin[w, s, f])

    lat_acc[...] = jnp.zeros_like(lat_acc)

    def add_latent(w, a, b):
        lat_acc[w] += dot_nt(afull[w, a, b], xin[w, a, b])

    def rs_nbr(w, axis, step):
        on_x = (axis == 0) == (w == 0)
        return (me_s, at(step, 0) if on_x else at(0, step))

    rs = {}

    def rs_send(key, w, i, step):
        m = msgs.make(gsend.at[w, i], grecv.at[w, i], rs_nbr(w, 0, step))
        m.start()
        rs[key] = m

    VIA = {0: 1, 1: 1, 2: -1, 3: -1}

    def rs_m1(w, s):
        gsend[w, s] = partial(w, 2, s).astype(BF16)
        rs_send((w, "m1", s), w, s, VIA[s])

    def rs_m2(w, s):
        f = (-VIA[s]) % SIDE
        gsend[w, 4 + s] = partial(w, f, s).astype(BF16)
        rs_send((w, "m2", s), w, 4 + s, -VIA[s])

    def rs_m3(w, s):
        f = VIA[s] % SIDE
        rs[(w, "m1", s)].wait_recv()
        gsend[w, 8 + s] = (partial(w, f, s) + grecv[w, s].astype(F32)).astype(BF16)
        rs_send((w, "m3", s), w, 8 + s, VIA[s])

    def rs_own(w, s):
        g = partial(w, 0, s)
        rs[(w, "m2", s)].wait_recv()
        rs[(w, "m3", s)].wait_recv()
        return g + grecv[w, 4 + s].astype(F32) + grecv[w, 8 + s].astype(F32)

    def rs2_send(key, w, i, step):
        m = msgs.make(hsend.at[w, i], hrecv.at[w, i], rs_nbr(w, 1, step))
        m.start()
        rs[key] = m

    order = []
    for h in range(2):
        order += [(3, 0, h), (1, 0, h)]
    for h in range(2):
        order += [(0, 3, h), (0, 1, h)]
    order += [(2, 0, 0), (2, 0, 1)]
    for a in (3, 1):
        for h in range(2):
            order += [(a, 3, h), (a, 1, h)]
    order += [(0, 2, 0), (0, 2, 1)]
    for h in range(2):
        order += [(2, 3, h), (2, 1, h)]
    for a in (3, 1, 2):
        order += [(a, 2, 0), (a, 2, 1)]
    todo = [(0, 0)]
    arrived = {}
    for n, (a, b, h) in enumerate(order):
        for w in range(WIN):
            ag[(w, a, b, h)].wait_recv()
            ag_on(w, a, b, h)
        arrived[(a, b)] = arrived.get((a, b), 0) + 1
        if todo:
            ta, tb = todo.pop(0)
            for w in range(WIN):
                add_latent(w, ta, tb)
        if arrived[(a, b)] == 2:
            todo.append((a, b))
        if 14 <= n < 18:
            s = (2, 3, 1, 0)[n - 14]
            for w in range(WIN):
                rs_m1(w, s)
        if 18 <= n < 22:
            s = (2, 3, 1, 0)[n - 18]
            for w in range(WIN):
                rs_m2(w, s)
    for ta, tb in todo:
        for w in range(WIN):
            add_latent(w, ta, tb)

    for w in range(WIN):
        lat[w] = lat_acc[w].astype(BF16)
    g0 = dot_nn(lat[0], cot[0]) * adapter_scale
    g1 = dot_nn(lat[1], cot[1]) * adapter_scale
    for d in range(N_DP):
        cols = slice(d * LK, (d + 1) * LK)
        gb_stage[d] = jnp.concatenate([g0[:, cols], g1[:, cols]], axis=1).astype(BF16)
    gb_recv[0] = gb_stage[me_d]
    gb_msgs = []
    for j in range(1, N_DP):
        to = (me_d + j) % N_DP
        m = msgs.make(gb_stage.at[to], gb_recv.at[j], (me_s, to))
        m.start()
        gb_msgs.append(m)

    for s in (2, 3, 1, 0):
        for w in range(WIN):
            rs_m3(w, s)

    outs = []

    def put(src, dst, i):
        c = pltpu.make_async_copy(src, dst, out_sem.at[i])
        c.start()
        outs.append(c)

    put(pa, pa_out, 0)
    put(pb, pb_out, 1)
    put(lat, lat_out, 2)
    put(bw, bw_out, 3)
    recv_all(bm_msgs)
    recv_all(m_msgs)
    for s in range(NEW_DEV):
        v = bm_recv[src_k[s]]
        pbm[s] = jnp.where(present[s], v, jnp.zeros_like(v))
        for i in range(2):
            v = m_recv[src_k[s], i]
            pm[s, i] = jnp.where(present[s], v, jnp.zeros_like(v))
    put(pbm, pbm_out, 4)
    put(pm, pm_out, 5)

    top, bottom = pl.ds(0, HALF), pl.ds(HALF, HALF)
    for w in range(WIN):
        g = rs_own(w, 2)
        hsend[w, 0] = g[:HALF].astype(BF16)
        rs2_send((w, "n1", 1), w, 0, 1)
        hsend[w, 1] = g[HALF:].astype(BF16)
        rs2_send((w, "n1", 3), w, 1, -1)
    for w in range(WIN):
        g = rs_own(w, 3)
        hsend[w, 2] = g[:HALF].astype(BF16)
        rs2_send((w, "n2", 3), w, 2, -1)
        hbuf[w, 0] = g[HALF:]
        g = rs_own(w, 1)
        hsend[w, 3] = g[HALF:].astype(BF16)
        rs2_send((w, "n2", 1), w, 3, 1)
        hbuf[w, 1] = g[:HALF]
    for w in range(WIN):
        rs[(w, "n1", 1)].wait_recv()
        hsend[w, 4] = (hbuf[w, 1] + hrecv[w, 0].astype(F32)).astype(BF16)
        rs2_send((w, "n3", 1), w, 4, 1)
        rs[(w, "n1", 3)].wait_recv()
        hsend[w, 5] = (hbuf[w, 0] + hrecv[w, 1].astype(F32)).astype(BF16)
        rs2_send((w, "n3", 3), w, 5, -1)
    for w in range(WIN):
        ga[w] = rs_own(w, 0)

    for m in gb_msgs:
        m.wait_recv()
    total = gb_recv[0].astype(F32)
    for j in range(1, N_DP):
        total += gb_recv[j].astype(F32)
    gb[...] = total
    put(gb, gb_out, 6)

    for w in range(WIN):
        rs[(w, "n2", 3)].wait_recv()
        rs[(w, "n3", 1)].wait_recv()
        ga[w, top] = adapter_scale * (
            ga[w, top] + hrecv[w, 2].astype(F32) + hrecv[w, 4].astype(F32)
        )
        rs[(w, "n2", 1)].wait_recv()
        rs[(w, "n3", 3)].wait_recv()
        ga[w, bottom] = adapter_scale * (
            ga[w, bottom] + hrecv[w, 3].astype(F32) + hrecv[w, 5].astype(F32)
        )
    put(ga, ga_out, 7)

    for group in (b_msgs, a_msgs[0], a_msgs[1], bm_msgs, m_msgs):
        wait_sent(group)
    for m in bg_msgs + gb_msgs + list(ag.values()) + list(rs.values()):
        m.wait_send()
    for c in outs:
        c.wait()
    assert msgs.count <= N_MSG


def exchange(*args):
    shape = jax.ShapeDtypeStruct
    anywhere = pl.BlockSpec(memory_space=pl.ANY)
    smem = pl.BlockSpec(memory_space=pltpu.SMEM)
    dma = pltpu.SemaphoreType.DMA
    V = pltpu.VMEM
    return pl.pallas_call(
        exchange_kernel,
        out_shape=(
            shape((NEW_DEV, R, LD), BF16),
            shape((NEW_DEV, 2, R, LD), BF16),
            shape((NEW_DEV, HALF, 2 * LK), BF16),
            shape((NEW_DEV, R, 2 * LK), BF16),
            shape((WIN, R, LD), F32),
            shape((R, 2 * LK), F32),
            shape((WIN, R, TOK), BF16),
            shape((WIN, R, KV), BF16),
        ),
        in_specs=[smem, smem] + [anywhere] * 8,
        out_specs=[anywhere] * 8,
        scratch_shapes=[
            V((WIN, SIDE, SIDE, TOK, LD), BF16),
            V((WIN, TOK, KV), BF16),
            V((OLD_DEV, R, LD), BF16),
            V((OLD_DEV, R, LD), F32),
            V((OLD_DEV, R, LD), F32),
            V((OLD_DEV, R, LK), BF16),
            V((OLD_DEV, R, LK), F32),
            V((OLD_DEV, R, LK), F32),
            V((N_SECTION, HALF, 2 * LK), BF16),
            V((N_SECTION, HALF, 2 * LK), BF16),
            V((N_SECTION, R, 2 * LK), BF16),
            V((N_SECTION, R, 2 * LK), BF16),
            V((N_SECTION, HALF, LD), BF16),
            V((N_SECTION, HALF, LD), BF16),
            V((N_SECTION, HALF, LD), BF16),
            V((N_SECTION, HALF, LD), BF16),
            V((N_SECTION, 2, R, LD), BF16),
            V((N_SECTION, 2, R, LD), BF16),
            V((WIN, SIDE, SIDE, R, LD), BF16),
            V((N_DP, R, 2 * LK), BF16),
            V((WIN, R, KV), BF16),
            V((WIN, R, TOK), BF16),
            V((WIN, R, TOK), F32),
            V((WIN, R, TOK), BF16),
            V((N_DP, R, 2 * LK), BF16),
            V((N_DP, R, 2 * LK), BF16),
            V((WIN, 12, R, LD), BF16),
            V((WIN, 12, R, LD), BF16),
            V((WIN, 2, HALF, LD), F32),
            V((WIN, 6, HALF, LD), BF16),
            V((WIN, 6, HALF, LD), BF16),
            V((NEW_DEV, R, LD), BF16),
            V((NEW_DEV, 2, R, LD), BF16),
            V((NEW_DEV, HALF, 2 * LK), BF16),
            V((NEW_DEV, R, 2 * LK), BF16),
            V((WIN, R, LD), F32),
            V((R, 2 * LK), F32),
            dma((N_MSG,)),
            dma((N_MSG,)),
            dma((8,)),
            dma((WIN, SIDE, SIDE)),
            dma((8,)),
        ],
        compiler_params=pltpu.CompilerParams(
            collective_id=0, has_side_effects=True, vmem_limit_bytes=56 * 1024 * 1024
        ),
    )(*args)


def adam(first, second, grad):
    first_new = beta_one * first + (1.0 - beta_one) * grad
    second_new = beta_two * second + (1.0 - beta_two) * grad * grad
    direction = first_new / corr_one / (jnp.sqrt(second_new / corr_two) + adam_eps)
    return first_new, second_new, direction


def finish_kernel(
    pa, pm, pb, pbm, ga, gb, lat, bw, out, new_a, new_b, fa, sa, fb, sb, step_a, step_b
):
    s = pl.program_id(0)
    new_a[...] = pa[...]
    v = pb[0].astype(F32)
    new_b[0] = jnp.concatenate([v[:, :LK], v[:, LK:]], axis=0).astype(BF16)
    first, second = pm[0, 0].astype(F32), pm[0, 1].astype(F32)
    bm = pbm[0].astype(F32)
    first_b, second_b = bm[:, :LK], bm[:, LK:]

    @pl.when(s < WIN)
    def _():
        f, q, d = adam(first, second, ga[0])
        fa[0], sa[0], step_a[0] = f, q, d
        g = gb[...]
        g = jnp.where(s == 0, g[:, :LK], g[:, LK:])
        f, q, d = adam(first_b, second_b, g)
        fb[0], sb[0], step_b[0] = f, q, d
        product = lax.dot_general(
            lat[0], bw[0], (((0,), (0,)), ((), ())), preferred_element_type=F32
        )
        out[0] = (adapter_scale * product).astype(BF16)

    @pl.when(s >= WIN)
    def _():
        fa[0], sa[0] = first, second
        fb[0], sb[0] = first_b, second_b


def finish(*args):
    shape = jax.ShapeDtypeStruct

    def every(*dims):
        return pl.BlockSpec((1,) + dims, lambda s: (s,) + (0,) * len(dims))

    def window(*dims):
        return pl.BlockSpec((1,) + dims, lambda s: (jnp.minimum(s, WIN - 1),) + (0,) * len(dims))

    return pl.pallas_call(
        finish_kernel,
        grid=(NEW_DEV,),
        out_shape=(
            shape((WIN, TOK, KV), BF16),
            shape((NEW_DEV, R, LD), BF16),
            shape((NEW_DEV, R, LK), BF16),
            shape((NEW_DEV, R, LD), F32),
            shape((NEW_DEV, R, LD), F32),
            shape((NEW_DEV, R, LK), F32),
            shape((NEW_DEV, R, LK), F32),
            shape((WIN, R, LD), F32),
            shape((WIN, R, LK), F32),
        ),
        in_specs=[
            every(R, LD),
            every(2, R, LD),
            every(HALF, 2 * LK),
            every(R, 2 * LK),
            window(R, LD),
            pl.BlockSpec((R, 2 * LK), lambda s: (0, 0)),
            window(R, TOK),
            window(R, KV),
        ],
        out_specs=[
            window(TOK, KV),
            every(R, LD),
            every(R, LK),
            every(R, LD),
            every(R, LD),
            every(R, LK),
            every(R, LK),
            window(R, LD),
            window(R, LK),
        ],
    )(*args)


def body(*args):
    return finish(*exchange(*args))


def solution(mesh):
    state = P("section", None, "dp")
    tokens = P("section", "dp", None)
    in_specs = (P(), P()) + (state,) * 6 + (tokens,) * 2
    out_specs = (tokens,) + (state,) * 8
    return jax.shard_map(body, mesh=mesh, in_specs=in_specs, out_specs=out_specs, check_vma=False)
```

```python
import jax
import jax.numpy as jnp
from jax import lax
from jax.experimental import pallas as pl
from jax.experimental.pallas import tpu as pltpu
from jax.sharding import PartitionSpec as P

MESH = pl.DeviceIdType.MESH
F32 = jnp.float32
BF16 = jnp.bfloat16

OLD_DEV = 3
NEW_DEV = 4
WIN = 2
LAYERS = 24
N_SECTION = 8
N_NEW = 6
N_DP = 16
SIDE = 4
R = 64
HALF = 32
CHUNKS = ((0, 16), (16, 48))
TOK = 256
LD = 1024
LK = 64
KV = 1024

adapter_scale = 2.0
beta_one = 0.9
beta_two = 0.999
adam_eps = 1e-08
corr_one = 1.0 - (0.9**10) ** 10
corr_two = 1.0 - (0.999**10) ** 10


def dot_nt(a, b):
    return lax.dot_general(a, b, (((1,), (1,)), ((), ())), preferred_element_type=F32)


def dot_nn(a, b):
    return jnp.dot(a, b, preferred_element_type=F32)


class Messages:
    def __init__(self, send_sem, recv_sem):
        self.send_sem, self.recv_sem = send_sem, recv_sem
        self.count = self.sends = 0

    def make(self, src, dst, device, send=None):
        i = self.count
        self.count += 1
        if send is None:
            send = self.send_sem.at[self.sends]
            self.sends += 1
        return pltpu.make_async_remote_copy(
            src_ref=src,
            dst_ref=dst,
            send_sem=send,
            recv_sem=self.recv_sem.at[i],
            device_id=device,
            device_id_type=MESH,
        )


N_SEND = 47
N_RECV = 143


def exchange_kernel(
    old_slot_hbm,
    new_slot_hbm,
    a_old,
    a_first_old,
    a_second_old,
    b_old,
    b_first_old,
    b_second_old,
    inputs,
    cotangent,
    pa_out,
    pm_out,
    pb_out,
    pbm_out,
    ga_out,
    gb_out,
    lat_out,
    bw_out,
    old_slot,
    new_slot,
    xin,
    cot,
    av,
    mv1,
    mv2,
    bv,
    bmv1,
    bmv2,
    b_stage,
    b_recv,
    bm_stage,
    bm_recv,
    a_stage0,
    a_stage1,
    a_recv0,
    a_recv1,
    m_stage,
    m_recv,
    afull,
    bfull,
    bw,
    pulled,
    lat_acc,
    lat,
    gb_stage,
    gb_recv,
    gb_half,
    gb_last,
    gsend,
    grecv,
    hbuf,
    hsend,
    hrecv,
    pa,
    pm,
    pb,
    pbm,
    ga,
    gb,
    send_sem,
    recv_sem,
    ring_sem,
    load_sem,
    x_sem,
    out_sem,
):
    me_s = lax.axis_index("section")
    me_d = lax.axis_index("dp")
    mx = me_d // SIDE
    mz = me_d % SIDE

    def at(dx, dz):
        return ((mx + dx) % SIDE) * SIDE + (mz + dz) % SIDE

    msgs = Messages(send_sem, recv_sem)

    def load(src, dst, i):
        c = pltpu.make_async_copy(src, dst, load_sem.at[i])
        c.start()
        return c

    row = [(me_s, at(j, 0)) for j in range(1, SIDE)]
    column = [(me_s, at(0, j)) for j in range(1, SIDE)]
    barrier = pltpu.get_barrier_semaphore()
    for k in range(1, N_SECTION):
        pl.semaphore_signal(
            barrier, inc=1, device_id=((me_s + k) % N_SECTION, me_d), device_id_type=MESH
        )
    for device in row + column:
        pl.semaphore_signal(barrier, inc=1, device_id=device, device_id_type=MESH)

    ld_old = load(old_slot_hbm, old_slot, 7)
    ld_new = load(new_slot_hbm, new_slot, 8)
    ld_a = load(a_old, av, 1)
    ld_b = load(b_old, bv, 0)
    ld_cot = load(cotangent, cot, 2)
    ld_b1 = load(b_first_old, bmv1, 3)
    ld_b2 = load(b_second_old, bmv2, 4)

    def x_copy(w, a, b):
        ax = at(b, a) if w == 0 else at(a, b)
        return pltpu.make_async_copy(
            inputs.at[w, :, pl.ds(pl.multiple_of(ax * LD, LD), LD)],
            xin.at[w, a, b],
            x_sem.at[w],
        )

    ld_old.wait()
    ld_new.wait()
    dest = []
    for j in range(OLD_DEV):
        total = jnp.int32(0)
        for l in range(LAYERS):
            total += jnp.where(old_slot[l] == me_s * OLD_DEV + j, new_slot[l] // NEW_DEV, 0)
        dest.append(total)
    src_k, present = [], []
    for s in range(NEW_DEV):
        total, has = jnp.int32(0), jnp.int32(0)
        for l in range(LAYERS):
            hit = new_slot[l] == me_s * NEW_DEV + s
            total += jnp.where(hit, old_slot[l] // OLD_DEV, 0)
            has += jnp.where(hit, 1, 0)
        src_k.append((me_s + N_SECTION - total) % N_SECTION)
        present.append(has > 0)
    send_index = []
    for k in range(N_SECTION):
        d = (me_s + k) % N_SECTION
        pick = jnp.int32(0)
        for j in range(1, OLD_DEV):
            pick = jnp.where(dest[j] == d, j, pick)
        send_index.append(pick)

    receives = me_s < N_NEW

    def peer(k):
        return ((me_s + k) % N_SECTION, me_d)

    def sends_to(k):
        return (me_s + k) % N_SECTION < N_NEW

    def pack_b(v):
        v = v.astype(F32)
        return jnp.concatenate([v[:HALF], v[HALF:]], axis=1).astype(BF16)

    @pl.when(jnp.logical_not(receives))
    def _():
        b_recv[...] = jnp.zeros_like(b_recv)
        bm_recv[...] = jnp.zeros_like(bm_recv)
        a_recv0[...] = jnp.zeros_like(a_recv0)
        a_recv1[...] = jnp.zeros_like(a_recv1)
        m_recv[...] = jnp.zeros_like(m_recv)

    def start_all(group):
        for k, m in group.items():
            @pl.when(sends_to(k))
            def _(m=m):
                m.start()

    def recv_all(group):
        @pl.when(receives)
        def _():
            for m in group.values():
                m.wait_recv()

    def wait_sent(group):
        for k, m in group.items():
            @pl.when(sends_to(k))
            def _(m=m):
                m.wait_send()

    a_stage, a_recv = (a_stage0, a_stage1), (a_recv0, a_recv1)
    a_msgs = [
        {k: msgs.make(a_stage[h].at[k], a_recv[h].at[k], peer(k)) for k in range(1, N_SECTION)}
        for h in range(2)
    ]

    def stage_a(h):
        start, size = CHUNKS[h]
        for k in range(N_SECTION):
            v = av[send_index[k], pl.ds(start, size), :]
            if k == 0:
                a_recv[h][0] = v
            else:
                a_stage[h][k] = v

    ld_a.wait()
    stage_a(0)
    ld_b.wait()
    for k in range(N_SECTION):
        v = pack_b(bv[send_index[k]])
        if k == 0:
            b_recv[0] = v
        else:
            b_stage[k] = v
    b_msgs = {
        k: msgs.make(b_stage.at[k], b_recv.at[k], peer(k)) for k in range(1, N_SECTION)
    }
    pl.semaphore_wait(barrier, N_SECTION - 1 + 2 * (SIDE - 1))
    start_all(b_msgs)
    start_all(a_msgs[0])
    stage_a(1)

    ld_m1 = load(a_first_old, mv1, 5)
    ld_m2 = load(a_second_old, mv2, 6)
    for w in range(WIN):
        for b in range(SIDE):
            for a in range(SIDE):
                x_copy(w, a, b).start()

    def nbr(w, axis, step):
        on_x = (axis == 1) == (w == 0)
        return (me_s, at(step, 0) if on_x else at(0, step))

    ag = {}
    PLUS, MINUS = 1, 3

    def ag_make(w, a, b, h, axis, step):
        na, nb = (a, b)
        if axis == 0:
            na = (a - step) % SIDE
        else:
            nb = (b - step) % SIDE
        rows = pl.ds(*CHUNKS[h])
        m = msgs.make(
            afull.at[w, a * SIDE + b, rows],
            afull.at[w, na * SIDE + nb, rows],
            nbr(w, axis, step),
            ring_sem.at[0, w],
        )
        assert (w, na, nb, h) not in ag
        ag[(w, na, nb, h)] = m
        m.start()

    def ag_on(w, a, b, h):
        if b == 0:
            if a == 0:
                ag_make(w, a, b, h, 0, 1)
                ag_make(w, a, b, h, 0, -1)
            elif a == 3 and h == 0:
                ag_make(w, a, b, h, 0, 1)
            elif a == 1 and h == 1:
                ag_make(w, a, b, h, 0, -1)
            ag_make(w, a, b, h, 1, 1)
            ag_make(w, a, b, h, 1, -1)
        elif b == 3 and h == a % 2:
            ag_make(w, a, b, h, 1, 1)
        elif b == 1 and h != a % 2:
            ag_make(w, a, b, h, 1, -1)

    def ag_own(h):
        rows = pl.ds(*CHUNKS[h])
        for s in range(NEW_DEV):
            v = a_recv[h][src_k[s]]
            v = jnp.where(present[s], v, jnp.zeros_like(v))
            pa[s, rows] = v
            if s < WIN:
                afull[s, 0, rows] = v
                ag_on(s, 0, 0, h)

    order = [(3, 0), (1, 0), (0, 3), (0, 1), (2, 0), (3, 3), (3, 1), (1, 3), (1, 1)]
    order += [(0, 2), (2, 3), (2, 1), (3, 2), (1, 2), (2, 2)]

    def ag_event(a, b, h):
        for w in range(WIN):
            ag[(w, a, b, h)].wait_recv()
            ag_on(w, a, b, h)

    recv_all(b_msgs)

    def unpack_b(v):
        v = v.astype(F32)
        return jnp.concatenate([v[:, :LK], v[:, LK:]], axis=0)

    pbs = []
    for s in range(NEW_DEV):
        v = b_recv[src_k[s]]
        v = jnp.where(present[s], v, jnp.zeros_like(v))
        pb[s] = v
        if s < WIN:
            pbs.append(unpack_b(v))
    bfull[mx, mz] = jnp.concatenate(pbs, axis=1).astype(BF16)
    bz_msgs, bx_msgs = [], []
    for device in column:
        m = msgs.make(bfull.at[mx, mz], bfull.at[mx, mz], device)
        m.start()
        bz_msgs.append(m)


    recv_all(a_msgs[0])
    start_all(a_msgs[1])
    ag_own(0)
    for m in bz_msgs:
        m.wait_recv()
    for device in row:
        m = msgs.make(bfull.at[mx], bfull.at[mx], device)
        m.start()
        bx_msgs.append(m)
    for a, b in order[:4]:
        ag_event(a, b, 0)

    for m in bx_msgs:
        m.wait_recv()
    for d in range(0, N_DP, 2):
        x, z = d // SIDE, d % SIDE
        lo, hi = bfull[x, z].astype(F32), bfull[x, z + 1].astype(F32)
        cols = pl.ds(d * LK, 2 * LK)
        bw[0, :, cols] = jnp.concatenate([lo[:, :LK], hi[:, :LK]], axis=1).astype(BF16)
        bw[1, :, cols] = jnp.concatenate([lo[:, LK:], hi[:, LK:]], axis=1).astype(BF16)
    ld_cot.wait()
    for w in range(WIN):
        pulled[w] = dot_nt(bw[w], cot[w]).astype(BF16)

    for w in range(WIN):
        pltpu.make_async_copy(xin.at[w], xin.at[w], x_sem.at[w]).wait()

    def partial(w, f, s):
        return dot_nn(pulled[w], xin[w, s, f])

    lat_acc[...] = jnp.zeros_like(lat_acc)

    def add_latent(w, a, b):
        lat_acc[w] += dot_nt(afull[w, a * SIDE + b], xin[w, a, b])

    def rs_nbr(w, axis, step):
        on_x = (axis == 0) == (w == 0)
        return (me_s, at(step, 0) if on_x else at(0, step))

    rs = {}

    def rs_send(key, w, i, step):
        m = msgs.make(gsend.at[w, i], grecv.at[w, i], rs_nbr(w, 0, step), ring_sem.at[1, w])
        m.start()
        rs[key] = m

    VIA = {0: 1, 1: 1, 2: -1, 3: -1}

    def rs_compute(w, s):
        gsend[w, s] = partial(w, 2, s).astype(BF16)
        gsend[w, 4 + s] = partial(w, (-VIA[s]) % SIDE, s).astype(BF16)

    def rs_start(s):
        for w in range(WIN):
            rs_send((w, "m1", s), w, s, VIA[s])
        for w in range(WIN):
            rs_send((w, "m2", s), w, 4 + s, -VIA[s])

    def rs_m3(w, s):
        f = VIA[s] % SIDE
        rs[(w, "m1", s)].wait_recv()
        gsend[w, 8 + s] = (partial(w, f, s) + grecv[w, s].astype(F32)).astype(BF16)
        rs_send((w, "m3", s), w, 8 + s, VIA[s])

    def rs_own(w, s):
        g = partial(w, 0, s)
        rs[(w, "m2", s)].wait_recv()
        rs[(w, "m3", s)].wait_recv()
        return g + grecv[w, 4 + s].astype(F32) + grecv[w, 8 + s].astype(F32)

    def rs2_send(key, w, i, step):
        m = msgs.make(hsend.at[w, i], hrecv.at[w, i], rs_nbr(w, 1, step), ring_sem.at[2, w])
        m.start()
        rs[key] = m

    top, bottom = pl.ds(0, HALF), pl.ds(HALF, HALF)

    def rs_n1(w):
        g = rs_own(w, 2)
        hsend[w, 0] = g[:HALF].astype(BF16)
        rs2_send((w, "n1", 1), w, 0, 1)
        hsend[w, 1] = g[HALF:].astype(BF16)
        rs2_send((w, "n1", 3), w, 1, -1)

    def rs_n2(w):
        g = rs_own(w, 3)
        hsend[w, 2] = g[:HALF].astype(BF16)
        rs2_send((w, "n2", 3), w, 2, -1)
        hbuf[w, 0] = g[HALF:]
        g = rs_own(w, 1)
        hsend[w, 3] = g[HALF:].astype(BF16)
        rs2_send((w, "n2", 1), w, 3, 1)
        hbuf[w, 1] = g[:HALF]

    def rs_n3(w):
        rs[(w, "n1", 1)].wait_recv()
        hsend[w, 4] = (hbuf[w, 1] + hrecv[w, 0].astype(F32)).astype(BF16)
        rs2_send((w, "n3", 1), w, 4, 1)
        rs[(w, "n1", 3)].wait_recv()
        hsend[w, 5] = (hbuf[w, 0] + hrecv[w, 1].astype(F32)).astype(BF16)
        rs2_send((w, "n3", 3), w, 5, -1)

    SUMS = (2, 3, 1, 0)
    todo = [(0, 0)]

    def latent_of_next():
        if todo:
            ta, tb = todo.pop(0)
            for w in range(WIN):
                add_latent(w, ta, tb)

    def early(blocks):
        for a, b in blocks:
            ag_event(a, b, 0)

    def late(blocks):
        for a, b in blocks:
            ag_event(a, b, 1)
            todo.append((a, b))

    def rs_first(s):
        for w in range(WIN):
            rs_compute(w, s)
        rs_start(s)

    def rs_add(s):
        for w in range(WIN):
            rs_m3(w, s)

    rs_first(SUMS[0])
    rs_first(SUMS[1])
    recv_all(a_msgs[1])
    ag_own(1)
    early(order[4:9])
    pass
    pass
    late(order[:4])

    ld_b1.wait()
    ld_b2.wait()
    ld_m1.wait()
    ld_m2.wait()
    for k in range(N_SECTION):
        bm = jnp.concatenate([bmv1[send_index[k]], bmv2[send_index[k]]], axis=1).astype(BF16)
        for i, mv in enumerate((mv1, mv2)):
            v = mv[send_index[k]].astype(BF16)
            if k == 0:
                m_recv[0, i] = v
            else:
                m_stage[k, i] = v
        if k == 0:
            bm_recv[0] = bm
        else:
            bm_stage[k] = bm
    bm_msgs = {
        k: msgs.make(bm_stage.at[k], bm_recv.at[k], peer(k)) for k in range(1, N_SECTION)
    }
    m_msgs = {k: msgs.make(m_stage.at[k], m_recv.at[k], peer(k)) for k in range(1, N_SECTION)}
    start_all(bm_msgs)
    start_all(m_msgs)


    early(order[9:])
    rs_add(SUMS[0])
    rs_first(SUMS[2])
    rs_add(SUMS[1])
    late(order[4:9])
    rs_first(SUMS[3])
    for w in range(WIN):
        rs_n1(w)
    rs_add(SUMS[2])
    for _ in range(4):
        latent_of_next()
    late(order[9:12])
    rs_add(SUMS[3])
    for _ in range(3):
        latent_of_next()
    for w in range(WIN):
        rs_n2(w)
    for _ in range(3):
        latent_of_next()
    late(order[12:])
    for w in range(WIN):
        rs_n3(w)
    for ta, tb in todo:
        for w in range(WIN):
            add_latent(w, ta, tb)

    for w in range(WIN):
        lat[w] = lat_acc[w].astype(BF16)
    g0 = dot_nn(lat[0], cot[0]) * adapter_scale
    g1 = dot_nn(lat[1], cot[1]) * adapter_scale
    for d in range(N_DP):
        cols = slice(d * LK, (d + 1) * LK)
        g = jnp.concatenate([g0[:, cols], g1[:, cols]], axis=1).astype(BF16)
        gb_stage[d // SIDE, d % SIDE] = g
    gx_msgs, gz_msgs = [], []
    for j in range(1, SIDE):
        m = msgs.make(gb_stage.at[(mx + j) % SIDE], gb_recv.at[j], row[j - 1])
        m.start()
        gx_msgs.append(m)
    outs = []

    def put(src, dst, i):
        c = pltpu.make_async_copy(src, dst, out_sem.at[i])
        c.start()
        outs.append(c)

    put(pa, pa_out, 0)
    put(pb, pb_out, 1)
    put(lat, lat_out, 2)
    put(bw, bw_out, 3)
    recv_all(bm_msgs)
    recv_all(m_msgs)
    for s in range(NEW_DEV):
        v = bm_recv[src_k[s]]
        pbm[s] = jnp.where(present[s], v, jnp.zeros_like(v))
        for i in range(2):
            v = m_recv[src_k[s], i]
            pm[s, i] = jnp.where(present[s], v, jnp.zeros_like(v))
    put(pbm, pbm_out, 4)
    put(pm, pm_out, 5)

    for m in gx_msgs:
        m.wait_recv()
    total = gb_stage[mx].astype(F32)
    for j in range(1, SIDE):
        total += gb_recv[j].astype(F32)
    gb_half[...] = total.astype(BF16)
    for j in range(1, SIDE):
        m = msgs.make(gb_half.at[(mz + j) % SIDE], gb_last.at[j], column[j - 1])
        m.start()
        gz_msgs.append(m)
    for w in range(WIN):
        ga[w] = rs_own(w, 0)

    for m in gz_msgs:
        m.wait_recv()
    total = gb_half[mz].astype(F32)
    for j in range(1, SIDE):
        total += gb_last[j].astype(F32)
    gb[...] = total
    put(gb, gb_out, 6)

    for w in range(WIN):
        rs[(w, "n2", 3)].wait_recv()
        rs[(w, "n3", 1)].wait_recv()
        ga[w, top] = adapter_scale * (
            ga[w, top] + hrecv[w, 2].astype(F32) + hrecv[w, 4].astype(F32)
        )
        rs[(w, "n2", 1)].wait_recv()
        rs[(w, "n3", 3)].wait_recv()
        ga[w, bottom] = adapter_scale * (
            ga[w, bottom] + hrecv[w, 3].astype(F32) + hrecv[w, 5].astype(F32)
        )
    put(ga, ga_out, 7)

    for group in (b_msgs, a_msgs[0], a_msgs[1], bm_msgs, m_msgs):
        wait_sent(group)
    small = bz_msgs + bx_msgs + gx_msgs + gz_msgs
    for m in small:
        m.wait_send()
    for w in range(WIN):
        for i, ref in enumerate((afull.at[w, pl.ds(0, N_DP - 1)], gsend.at[w], hsend.at[w])):
            pltpu.make_async_remote_copy(
                src_ref=ref,
                dst_ref=ref,
                send_sem=ring_sem.at[i, w],
                recv_sem=recv_sem.at[0],
                device_id=row[0],
                device_id_type=MESH,
            ).wait_send()
    for c in outs:
        c.wait()
    assert (msgs.sends, msgs.count) == (N_SEND, N_RECV)


def exchange(*args):
    shape = jax.ShapeDtypeStruct
    anywhere = pl.BlockSpec(memory_space=pl.ANY)
    dma = pltpu.SemaphoreType.DMA
    V = pltpu.VMEM
    return pl.pallas_call(
        exchange_kernel,
        out_shape=(
            shape((NEW_DEV, R, LD), BF16),
            shape((NEW_DEV, 2, R, LD), BF16),
            shape((NEW_DEV, HALF, 2 * LK), BF16),
            shape((NEW_DEV, R, 2 * LK), BF16),
            shape((WIN, R, LD), F32),
            shape((R, 2 * LK), F32),
            shape((WIN, R, TOK), BF16),
            shape((WIN, R, KV), BF16),
        ),
        in_specs=[anywhere] * 10,
        out_specs=[anywhere] * 8,
        scratch_shapes=[
            pltpu.SMEM((LAYERS,), jnp.int32),
            pltpu.SMEM((LAYERS,), jnp.int32),
            V((WIN, SIDE, SIDE, TOK, LD), BF16),
            V((WIN, TOK, KV), BF16),
            V((OLD_DEV, R, LD), BF16),
            V((OLD_DEV, R, LD), F32),
            V((OLD_DEV, R, LD), F32),
            V((OLD_DEV, R, LK), BF16),
            V((OLD_DEV, R, LK), F32),
            V((OLD_DEV, R, LK), F32),
            V((N_SECTION, HALF, 2 * LK), BF16),
            V((N_SECTION, HALF, 2 * LK), BF16),
            V((N_SECTION, R, 2 * LK), BF16),
            V((N_SECTION, R, 2 * LK), BF16),
            V((N_SECTION, CHUNKS[0][1], LD), BF16),
            V((N_SECTION, CHUNKS[1][1], LD), BF16),
            V((N_SECTION, CHUNKS[0][1], LD), BF16),
            V((N_SECTION, CHUNKS[1][1], LD), BF16),
            V((N_SECTION, 2, R, LD), BF16),
            V((N_SECTION, 2, R, LD), BF16),
            V((WIN, N_DP, R, LD), BF16),
            V((SIDE, SIDE, R, 2 * LK), BF16),
            V((WIN, R, KV), BF16),
            V((WIN, R, TOK), BF16),
            V((WIN, R, TOK), F32),
            V((WIN, R, TOK), BF16),
            V((SIDE, SIDE, R, 2 * LK), BF16),
            V((SIDE, SIDE, R, 2 * LK), BF16),
            V((SIDE, R, 2 * LK), BF16),
            V((SIDE, R, 2 * LK), BF16),
            V((WIN, 12, R, LD), BF16),
            V((WIN, 12, R, LD), BF16),
            V((WIN, 2, HALF, LD), F32),
            V((WIN, 6, HALF, LD), BF16),
            V((WIN, 6, HALF, LD), BF16),
            V((NEW_DEV, R, LD), BF16),
            V((NEW_DEV, 2, R, LD), BF16),
            V((NEW_DEV, HALF, 2 * LK), BF16),
            V((NEW_DEV, R, 2 * LK), BF16),
            V((WIN, R, LD), F32),
            V((R, 2 * LK), F32),
            dma((N_SEND,)),
            dma((N_RECV,)),
            dma((3, WIN)),
            dma((9,)),
            dma((WIN,)),
            dma((8,)),
        ],
        compiler_params=pltpu.CompilerParams(
            collective_id=0, has_side_effects=True, vmem_limit_bytes=56 * 1024 * 1024
        ),
    )(*args)


def adam(first, second, grad):
    first_new = beta_one * first + (1.0 - beta_one) * grad
    second_new = beta_two * second + (1.0 - beta_two) * grad * grad
    size = jnp.sqrt(second_new * (1.0 / corr_two)) + adam_eps
    return first_new, second_new, first_new * (1.0 / corr_one) / size


def finish_kernel(
    pa,
    pm,
    pb,
    pbm,
    ga,
    gb,
    lat,
    bw,
    out,
    new_a,
    new_b,
    fa,
    sa,
    fb,
    sb,
    step_a,
    step_b,
    pa_v,
    pm_v,
    pb_v,
    pbm_v,
    ga_v,
    gb_v,
    lat_v,
    bw_v,
    out_v,
    new_b_v,
    fa_v,
    sa_v,
    fb_v,
    sb_v,
    step_a_v,
    step_b_v,
    in_sem,
    out_sem,
):
    def copy(src, dst, sem):
        c = pltpu.make_async_copy(src, dst, sem)
        c.start()
        return c

    outs = []

    def put(src, dst):
        outs.append(copy(src, dst, out_sem.at[len(outs)]))

    ld_pm = {}
    for i, s in enumerate((2, 3, 0, 1)):
        ld_pm[s] = copy(pm.at[s], pm_v.at[s], in_sem.at[i])
    ld_ga = [copy(ga.at[w], ga_v.at[w], in_sem.at[4 + w]) for w in range(WIN)]
    ld_lat = copy(lat, lat_v, in_sem.at[6])
    ld_bw = copy(bw, bw_v, in_sem.at[7])
    ld_pb = copy(pb, pb_v, in_sem.at[8])
    ld_pbm = copy(pbm, pbm_v, in_sem.at[9])
    ld_gb = copy(gb, gb_v, in_sem.at[10])
    ld_pa = copy(pa, pa_v, in_sem.at[11])

    ld_pa.wait()
    put(pa_v, new_a)
    for s in (2, 3):
        ld_pm[s].wait()
        fa_v[s] = pm_v[s, 0].astype(F32)
        put(fa_v.at[s], fa.at[s])
        sa_v[s] = pm_v[s, 1].astype(F32)
        put(sa_v.at[s], sa.at[s])
    for w in range(WIN):
        ld_pm[w].wait()
        ld_ga[w].wait()
        f, q, d = adam(pm_v[w, 0].astype(F32), pm_v[w, 1].astype(F32), ga_v[w])
        fa_v[w] = f
        put(fa_v.at[w], fa.at[w])
        sa_v[w] = q
        put(sa_v.at[w], sa.at[w])
        step_a_v[w] = d
        put(step_a_v.at[w], step_a.at[w])
    ld_lat.wait()
    ld_bw.wait()
    for w in range(WIN):
        product = lax.dot_general(
            lat_v[w], bw_v[w], (((0,), (0,)), ((), ())), preferred_element_type=F32
        )
        out_v[w] = (adapter_scale * product).astype(BF16)
        put(out_v.at[w], out.at[w])
    ld_pb.wait()
    ld_pbm.wait()
    ld_gb.wait()
    for s in range(NEW_DEV):
        v = pb_v[s].astype(F32)
        new_b_v[s] = jnp.concatenate([v[:, :LK], v[:, LK:]], axis=0).astype(BF16)
        bm = pbm_v[s].astype(F32)
        f, q = bm[:, :LK], bm[:, LK:]
        if s < WIN:
            f, q, step_b_v[s] = adam(f, q, gb_v[:, s * LK : (s + 1) * LK])
        fb_v[s], sb_v[s] = f, q
    put(new_b_v, new_b)
    put(fb_v, fb)
    put(sb_v, sb)
    put(step_b_v, step_b)
    for c in outs:
        c.wait()


def finish(*args):
    shape = jax.ShapeDtypeStruct
    anywhere = pl.BlockSpec(memory_space=pl.ANY)
    V = pltpu.VMEM
    return pl.pallas_call(
        finish_kernel,
        out_shape=(
            shape((WIN, TOK, KV), BF16),
            shape((NEW_DEV, R, LD), BF16),
            shape((NEW_DEV, R, LK), BF16),
            shape((NEW_DEV, R, LD), F32),
            shape((NEW_DEV, R, LD), F32),
            shape((NEW_DEV, R, LK), F32),
            shape((NEW_DEV, R, LK), F32),
            shape((WIN, R, LD), F32),
            shape((WIN, R, LK), F32),
        ),
        in_specs=[anywhere] * 8,
        out_specs=[anywhere] * 9,
        scratch_shapes=[
            V((NEW_DEV, R, LD), BF16),
            V((NEW_DEV, 2, R, LD), BF16),
            V((NEW_DEV, HALF, 2 * LK), BF16),
            V((NEW_DEV, R, 2 * LK), BF16),
            V((WIN, R, LD), F32),
            V((R, 2 * LK), F32),
            V((WIN, R, TOK), BF16),
            V((WIN, R, KV), BF16),
            V((WIN, TOK, KV), BF16),
            V((NEW_DEV, R, LK), BF16),
            V((NEW_DEV, R, LD), F32),
            V((NEW_DEV, R, LD), F32),
            V((NEW_DEV, R, LK), F32),
            V((NEW_DEV, R, LK), F32),
            V((WIN, R, LD), F32),
            V((WIN, R, LK), F32),
            pltpu.SemaphoreType.DMA((12,)),
            pltpu.SemaphoreType.DMA((17,)),
        ],
        compiler_params=pltpu.CompilerParams(vmem_limit_bytes=56 * 1024 * 1024),
    )(*args)


def body(*args):
    return finish(*exchange(*args))


def solution(mesh):
    state = P("section", None, "dp")
    tokens = P("section", "dp", None)
    in_specs = (P(), P()) + (state,) * 6 + (tokens,) * 2
    out_specs = (tokens,) + (state,) * 8
    return jax.shard_map(body, mesh=mesh, in_specs=in_specs, out_specs=out_specs, check_vma=False)
```

```python
import jax
import jax.numpy as jnp
from jax import lax
from jax.experimental import pallas as pl
from jax.experimental.pallas import tpu as pltpu
from jax.sharding import PartitionSpec as P

MESH = pl.DeviceIdType.MESH
F32 = jnp.float32
BF16 = jnp.bfloat16

OLD_DEV = 3
NEW_DEV = 4
WIN = 2
LAYERS = 24
N_SECTION = 8
N_NEW = 6
N_DP = 16
SIDE = 4
R = 64
HALF = 32
CHUNKS = ((0, 16), (16, 48))
TOK = 256
LD = 1024
LK = 64
KV = 1024

adapter_scale = 2.0
beta_one = 0.9
beta_two = 0.999
adam_eps = 1e-08
corr_one = 1.0 - (0.9**10) ** 10
corr_two = 1.0 - (0.999**10) ** 10


def dot_nt(a, b):
    return lax.dot_general(a, b, (((1,), (1,)), ((), ())), preferred_element_type=F32)


def dot_nn(a, b):
    return jnp.dot(a, b, preferred_element_type=F32)


class Messages:
    def __init__(self, send_sem, recv_sem):
        self.send_sem, self.recv_sem = send_sem, recv_sem
        self.count = self.sends = 0

    def make(self, src, dst, device, send=None, receive=None):
        if receive is None:
            receive = self.recv_sem.at[self.count]
            self.count += 1
        if send is None:
            send = self.send_sem.at[self.sends]
            self.sends += 1
        return pltpu.make_async_remote_copy(
            src_ref=src,
            dst_ref=dst,
            send_sem=send,
            recv_sem=receive,
            device_id=device,
            device_id_type=MESH,
        )


SCHEDULE = ("F0", "F1", "own", "E1", "L0", "moments", "E2", "A0", "F2", "A1", "P2", "L1", "F3")
SCHEDULE += ("N1", "A2", "P5", "L2", "A3", "P4", "N2", "P3", "L3", "N3", "gb", "gc", "place")
N_SEND = 12
N_RECV = 108


def exchange_kernel(
    old_slot_hbm,
    new_slot_hbm,
    a_old,
    a_first_old,
    a_second_old,
    b_old,
    b_first_old,
    b_second_old,
    inputs,
    cotangent,
    pa_out,
    pm_out,
    pb_out,
    pbm_out,
    ga_out,
    gb_out,
    lat_out,
    bw_out,
    old_slot,
    new_slot,
    xin,
    cot,
    av,
    mv1,
    mv2,
    bv,
    bmv1,
    bmv2,
    b_stage,
    b_recv,
    bm_stage,
    bm_recv,
    a_stage0,
    a_stage1,
    a_recv0,
    a_recv1,
    m_stage,
    m_recv,
    afull,
    bfull,
    bw,
    pulled,
    lat_acc,
    lat,
    gb_stage,
    gb_recv,
    gb_half,
    gb_last,
    gsend,
    grecv,
    hbuf,
    hsend,
    hrecv,
    pa,
    pm,
    pb,
    pbm,
    ga,
    gb,
    send_sem,
    recv_sem,
    ring_sem,
    section_sem,
    load_sem,
    x_sem,
    out_sem,
):
    me_s = lax.axis_index("section")
    me_d = lax.axis_index("dp")
    mx = me_d // SIDE
    mz = me_d % SIDE

    def at(dx, dz):
        return ((mx + dx) % SIDE) * SIDE + (mz + dz) % SIDE

    msgs = Messages(send_sem, recv_sem)

    def load(src, dst, i):
        c = pltpu.make_async_copy(src, dst, load_sem.at[i])
        c.start()
        return c

    row = [(me_s, at(j, 0)) for j in range(1, SIDE)]
    column = [(me_s, at(0, j)) for j in range(1, SIDE)]
    barrier = pltpu.get_barrier_semaphore()
    for k in range(1, N_SECTION):
        pl.semaphore_signal(
            barrier, inc=1, device_id=((me_s + k) % N_SECTION, me_d), device_id_type=MESH
        )
    for device in row + column:
        pl.semaphore_signal(barrier, inc=1, device_id=device, device_id_type=MESH)

    ld_old = load(old_slot_hbm, old_slot, 7)
    ld_new = load(new_slot_hbm, new_slot, 8)
    ld_a = load(a_old, av, 1)
    ld_b = load(b_old, bv, 0)
    ld_cot = load(cotangent, cot, 2)
    ld_b1 = load(b_first_old, bmv1, 3)
    ld_b2 = load(b_second_old, bmv2, 4)
    ld_m1 = load(a_first_old, mv1, 5)
    ld_m2 = load(a_second_old, mv2, 6)

    def x_copy(w, a, b):
        ax = at(b, a) if w == 0 else at(a, b)
        return pltpu.make_async_copy(
            inputs.at[w, :, pl.ds(pl.multiple_of(ax * LD, LD), LD)],
            xin.at[w, a, b],
            x_sem.at[w],
        )

    ld_old.wait()
    ld_new.wait()
    dest = []
    for j in range(OLD_DEV):
        total = jnp.int32(0)
        for l in range(LAYERS):
            total += jnp.where(old_slot[l] == me_s * OLD_DEV + j, new_slot[l] // NEW_DEV, 0)
        dest.append(total)
    src_k, present = [], []
    for s in range(NEW_DEV):
        total, has = jnp.int32(0), jnp.int32(0)
        for l in range(LAYERS):
            hit = new_slot[l] == me_s * NEW_DEV + s
            total += jnp.where(hit, old_slot[l] // OLD_DEV, 0)
            has += jnp.where(hit, 1, 0)
        src_k.append((me_s + N_SECTION - total) % N_SECTION)
        present.append(has > 0)
    send_index = []
    for k in range(N_SECTION):
        d = (me_s + k) % N_SECTION
        pick = jnp.int32(0)
        for j in range(1, OLD_DEV):
            pick = jnp.where(dest[j] == d, j, pick)
        send_index.append(pick)

    receives = me_s < N_NEW

    def peer(k):
        return ((me_s + k) % N_SECTION, me_d)

    def sends_to(k):
        return (me_s + k) % N_SECTION < N_NEW

    def pack_b(v):
        v = v.astype(F32)
        return jnp.concatenate([v[:HALF], v[HALF:]], axis=1).astype(BF16)

    @pl.when(jnp.logical_not(receives))
    def _():
        b_recv[...] = jnp.zeros_like(b_recv)
        bm_recv[...] = jnp.zeros_like(bm_recv)
        a_recv0[...] = jnp.zeros_like(a_recv0)
        a_recv1[...] = jnp.zeros_like(a_recv1)
        m_recv[...] = jnp.zeros_like(m_recv)

    class Group:
        def __init__(self, i, stage, landing):
            self.i, self.stage, self.landing = i, stage, landing

        def message(self, k, first, size):
            return msgs.make(
                self.stage.at[pl.ds(first, size)],
                self.landing.at[pl.ds(first, size)],
                peer(k),
                section_sem.at[0, self.i],
                section_sem.at[1, self.i],
            )

    def start_all(group):
        for k in range(1, N_SECTION):
            @pl.when(sends_to(k))
            def _(k=k):
                group.message(k, k, 1).start()

    def recv_all(group):
        @pl.when(receives)
        def _():
            group.message(1, 1, N_SECTION - 1).wait_recv()

    def wait_sent(group):
        @pl.when(receives)
        def _():
            group.message(1, 1, N_NEW - 1).wait_send()

        @pl.when(jnp.logical_not(receives))
        def _():
            group.message(1, 1, N_NEW).wait_send()

    a_stage, a_recv = (a_stage0, a_stage1), (a_recv0, a_recv1)
    a_msgs = [Group(h, a_stage[h], a_recv[h]) for h in range(2)]

    def stage_a(h):
        start, size = CHUNKS[h]
        for k in range(N_SECTION):
            v = av[send_index[k], pl.ds(start, size), :]
            if k == 0:
                a_recv[h][0] = v
            else:
                a_stage[h][k] = v

    ld_a.wait()
    stage_a(0)
    ld_b.wait()
    for k in range(N_SECTION):
        v = pack_b(bv[send_index[k]])
        if k == 0:
            b_recv[0] = v
        else:
            b_stage[k] = v
    b_msgs = Group(2, b_stage, b_recv)
    pl.semaphore_wait(barrier, N_SECTION - 1 + 2 * (SIDE - 1))
    start_all(b_msgs)
    start_all(a_msgs[0])
    stage_a(1)

    for w in range(WIN):
        for b in range(SIDE):
            for a in range(SIDE):
                x_copy(w, a, b).start()

    ld_b1.wait()
    ld_b2.wait()
    ld_m1.wait()
    ld_m2.wait()
    for k in range(N_SECTION):
        bm = jnp.concatenate([bmv1[send_index[k]], bmv2[send_index[k]]], axis=1).astype(BF16)
        for i, mv in enumerate((mv1, mv2)):
            v = mv[send_index[k]].astype(BF16)
            if k == 0:
                m_recv[0, i] = v
            else:
                m_stage[k, i] = v
        if k == 0:
            bm_recv[0] = bm
        else:
            bm_stage[k] = bm
    bm_msgs = Group(3, bm_stage, bm_recv)
    m_msgs = Group(4, m_stage, m_recv)

    def nbr(w, axis, step):
        on_x = (axis == 1) == (w == 0)
        return (me_s, at(step, 0) if on_x else at(0, step))

    ag = {}
    PLUS, MINUS = 1, 3

    def ag_make(w, a, b, h, axis, step):
        na, nb = (a, b)
        if axis == 0:
            na = (a - step) % SIDE
        else:
            nb = (b - step) % SIDE
        rows = pl.ds(*CHUNKS[h])
        m = msgs.make(
            afull.at[w, a * SIDE + b, rows],
            afull.at[w, na * SIDE + nb, rows],
            nbr(w, axis, step),
            ring_sem.at[0, w],
        )
        assert (w, na, nb, h) not in ag
        ag[(w, na, nb, h)] = m
        m.start()

    def ag_on(w, a, b, h):
        if b == 0:
            if a == 0:
                ag_make(w, a, b, h, 0, 1)
                ag_make(w, a, b, h, 0, -1)
            elif a == 3 and h == 0:
                ag_make(w, a, b, h, 0, 1)
            elif a == 1 and h == 1:
                ag_make(w, a, b, h, 0, -1)
            ag_make(w, a, b, h, 1, 1)
            ag_make(w, a, b, h, 1, -1)
        elif b == 3 and h == a % 2:
            ag_make(w, a, b, h, 1, 1)
        elif b == 1 and h != a % 2:
            ag_make(w, a, b, h, 1, -1)

    def ag_own(h):
        rows = pl.ds(*CHUNKS[h])
        for s in range(NEW_DEV):
            v = a_recv[h][src_k[s]]
            v = jnp.where(present[s], v, jnp.zeros_like(v))
            pa[s, rows] = v
            if s < WIN:
                afull[s, 0, rows] = v
                ag_on(s, 0, 0, h)

    order = [(3, 0), (1, 0), (0, 3), (0, 1), (2, 0), (3, 3), (3, 1), (1, 3), (1, 1)]
    order += [(0, 2), (2, 3), (2, 1), (3, 2), (1, 2), (2, 2)]

    def ag_event(a, b, h):
        for w in range(WIN):
            ag[(w, a, b, h)].wait_recv()
            ag_on(w, a, b, h)

    recv_all(b_msgs)

    def unpack_b(v):
        v = v.astype(F32)
        return jnp.concatenate([v[:, :LK], v[:, LK:]], axis=0)

    pbs = []
    for s in range(NEW_DEV):
        v = b_recv[src_k[s]]
        v = jnp.where(present[s], v, jnp.zeros_like(v))
        pb[s] = v
        if s < WIN:
            pbs.append(unpack_b(v))
    bfull[mx, mz] = jnp.concatenate(pbs, axis=1).astype(BF16)
    bz_msgs, bx_msgs = [], []
    for device in column:
        m = msgs.make(bfull.at[mx, mz], bfull.at[mx, mz], device)
        m.start()
        bz_msgs.append(m)


    recv_all(a_msgs[0])
    start_all(a_msgs[1])
    ag_own(0)
    for m in bz_msgs:
        m.wait_recv()
    for device in row:
        m = msgs.make(bfull.at[mx], bfull.at[mx], device)
        m.start()
        bx_msgs.append(m)
    for a, b in order[:4]:
        ag_event(a, b, 0)

    for m in bx_msgs:
        m.wait_recv()
    for d in range(0, N_DP, 2):
        x, z = d // SIDE, d % SIDE
        lo, hi = bfull[x, z].astype(F32), bfull[x, z + 1].astype(F32)
        cols = pl.ds(d * LK, 2 * LK)
        bw[0, :, cols] = jnp.concatenate([lo[:, :LK], hi[:, :LK]], axis=1).astype(BF16)
        bw[1, :, cols] = jnp.concatenate([lo[:, LK:], hi[:, LK:]], axis=1).astype(BF16)
    ld_cot.wait()
    for w in range(WIN):
        pulled[w] = dot_nt(bw[w], cot[w]).astype(BF16)

    for w in range(WIN):
        pltpu.make_async_copy(xin.at[w], xin.at[w], x_sem.at[w]).wait()

    def partial(w, f, s):
        return dot_nn(pulled[w], xin[w, s, f])

    lat_acc[...] = jnp.zeros_like(lat_acc)

    def add_latent(w, a, b):
        lat_acc[w] += dot_nt(afull[w, a * SIDE + b], xin[w, a, b])

    def rs_nbr(w, axis, step):
        on_x = (axis == 0) == (w == 0)
        return (me_s, at(step, 0) if on_x else at(0, step))

    rs = {}

    def rs_send(key, w, i, step):
        m = msgs.make(gsend.at[w, i], grecv.at[w, i], rs_nbr(w, 0, step), ring_sem.at[1, w])
        m.start()
        rs[key] = m

    VIA = {0: 1, 1: 1, 2: -1, 3: -1}

    def rs_compute(w, s):
        gsend[w, s] = partial(w, 2, s).astype(BF16)
        gsend[w, 4 + s] = partial(w, (-VIA[s]) % SIDE, s).astype(BF16)

    def rs_start(s):
        for w in range(WIN):
            rs_send((w, "m1", s), w, s, VIA[s])
        for w in range(WIN):
            rs_send((w, "m2", s), w, 4 + s, -VIA[s])

    def rs_m3(w, s):
        f = VIA[s] % SIDE
        rs[(w, "m1", s)].wait_recv()
        gsend[w, 8 + s] = (partial(w, f, s) + grecv[w, s].astype(F32)).astype(BF16)
        rs_send((w, "m3", s), w, 8 + s, VIA[s])

    def rs_own(w, s):
        g = partial(w, 0, s)
        rs[(w, "m2", s)].wait_recv()
        rs[(w, "m3", s)].wait_recv()
        return g + grecv[w, 4 + s].astype(F32) + grecv[w, 8 + s].astype(F32)

    def rs2_send(key, w, i, step):
        m = msgs.make(hsend.at[w, i], hrecv.at[w, i], rs_nbr(w, 1, step), ring_sem.at[2, w])
        m.start()
        rs[key] = m

    top, bottom = pl.ds(0, HALF), pl.ds(HALF, HALF)

    def rs_n1(w):
        g = rs_own(w, 2)
        hsend[w, 0] = g[:HALF].astype(BF16)
        rs2_send((w, "n1", 1), w, 0, 1)
        hsend[w, 1] = g[HALF:].astype(BF16)
        rs2_send((w, "n1", 3), w, 1, -1)

    def rs_n2(w):
        g = rs_own(w, 3)
        hsend[w, 2] = g[:HALF].astype(BF16)
        rs2_send((w, "n2", 3), w, 2, -1)
        hbuf[w, 0] = g[HALF:]
        g = rs_own(w, 1)
        hsend[w, 3] = g[HALF:].astype(BF16)
        rs2_send((w, "n2", 1), w, 3, 1)
        hbuf[w, 1] = g[:HALF]

    def rs_n3(w):
        rs[(w, "n1", 1)].wait_recv()
        hsend[w, 4] = (hbuf[w, 1] + hrecv[w, 0].astype(F32)).astype(BF16)
        rs2_send((w, "n3", 1), w, 4, 1)
        rs[(w, "n1", 3)].wait_recv()
        hsend[w, 5] = (hbuf[w, 0] + hrecv[w, 1].astype(F32)).astype(BF16)
        rs2_send((w, "n3", 3), w, 5, -1)

    SUMS = (2, 3, 1, 0)
    todo = [(0, 0)]

    def latent_of_next():
        if todo:
            ta, tb = todo.pop(0)
            for w in range(WIN):
                add_latent(w, ta, tb)

    def early(blocks):
        for a, b in blocks:
            ag_event(a, b, 0)

    def late(blocks):
        for a, b in blocks:
            ag_event(a, b, 1)
            todo.append((a, b))

    def rs_first(s):
        for w in range(WIN):
            rs_compute(w, s)
        rs_start(s)

    def rs_add(s):
        for w in range(WIN):
            rs_m3(w, s)

    gx_msgs, gz_msgs, outs = [], [], []

    def gb_rows():
        while todo:
            latent_of_next()
        for w in range(WIN):
            lat[w] = lat_acc[w].astype(BF16)
        g0 = dot_nn(lat[0], cot[0]) * adapter_scale
        g1 = dot_nn(lat[1], cot[1]) * adapter_scale
        for d in range(N_DP):
            cols = slice(d * LK, (d + 1) * LK)
            g = jnp.concatenate([g0[:, cols], g1[:, cols]], axis=1).astype(BF16)
            gb_stage[d // SIDE, d % SIDE] = g
        for j in range(1, SIDE):
            m = msgs.make(gb_stage.at[(mx + j) % SIDE], gb_recv.at[j], row[j - 1])
            m.start()
            gx_msgs.append(m)

    def gb_columns():
        for m in gx_msgs:
            m.wait_recv()
        total = gb_stage[mx].astype(F32)
        for j in range(1, SIDE):
            total += gb_recv[j].astype(F32)
        gb_half[...] = total.astype(BF16)
        for j in range(1, SIDE):
            m = msgs.make(gb_half.at[(mz + j) % SIDE], gb_last.at[j], column[j - 1])
            m.start()
            gz_msgs.append(m)

    def put(src, dst, i):
        c = pltpu.make_async_copy(src, dst, out_sem.at[i])
        c.start()
        outs.append(c)

    def place_moments():
        recv_all(bm_msgs)
        recv_all(m_msgs)
        for s in range(NEW_DEV):
            v = bm_recv[src_k[s]]
            pbm[s] = jnp.where(present[s], v, jnp.zeros_like(v))
            for i in range(2):
                v = m_recv[src_k[s], i]
                pm[s, i] = jnp.where(present[s], v, jnp.zeros_like(v))
        put(pa, pa_out, 0)
        put(pb, pb_out, 1)
        put(pbm, pbm_out, 4)
        put(pm, pm_out, 5)

    def own_late():
        recv_all(a_msgs[1])
        ag_own(1)

    def send_moments():
        start_all(bm_msgs)
        start_all(m_msgs)

    def both(step):
        for w in range(WIN):
            step(w)

    steps = {
        "own": own_late,
        "moments": send_moments,
        "E1": lambda: early(order[4:9]),
        "E2": lambda: early(order[9:]),
        "L0": lambda: late(order[:4]),
        "L1": lambda: late(order[4:9]),
        "L2": lambda: late(order[9:12]),
        "L3": lambda: late(order[12:]),
        "N1": lambda: both(rs_n1),
        "N2": lambda: both(rs_n2),
        "N3": lambda: both(rs_n3),
        "gb": gb_rows,
        "gc": gb_columns,
        "place": place_moments,
    }
    for i in range(SIDE):
        steps[f"F{i}"] = lambda i=i: rs_first(SUMS[i])
        steps[f"A{i}"] = lambda i=i: rs_add(SUMS[i])
    for step in SCHEDULE:
        if step[0] == "P":
            for _ in range(int(step[1:])):
                latent_of_next()
        else:
            steps[step]()
    put(lat, lat_out, 2)
    put(bw, bw_out, 3)
    for w in range(WIN):
        ga[w] = rs_own(w, 0)
    for m in gz_msgs:
        m.wait_recv()
    total = gb_half[mz].astype(F32)
    for j in range(1, SIDE):
        total += gb_last[j].astype(F32)
    gb[...] = total
    put(gb, gb_out, 6)

    for w in range(WIN):
        rs[(w, "n2", 3)].wait_recv()
        rs[(w, "n3", 1)].wait_recv()
        ga[w, top] = adapter_scale * (
            ga[w, top] + hrecv[w, 2].astype(F32) + hrecv[w, 4].astype(F32)
        )
        rs[(w, "n2", 1)].wait_recv()
        rs[(w, "n3", 3)].wait_recv()
        ga[w, bottom] = adapter_scale * (
            ga[w, bottom] + hrecv[w, 3].astype(F32) + hrecv[w, 5].astype(F32)
        )
    put(ga, ga_out, 7)

    for group in (b_msgs, a_msgs[0], a_msgs[1], bm_msgs, m_msgs):
        wait_sent(group)
    small = bz_msgs + bx_msgs + gx_msgs + gz_msgs
    for m in small:
        m.wait_send()
    for w in range(WIN):
        for i, ref in enumerate((afull.at[w, pl.ds(0, N_DP - 1)], gsend.at[w], hsend.at[w])):
            pltpu.make_async_remote_copy(
                src_ref=ref,
                dst_ref=ref,
                send_sem=ring_sem.at[i, w],
                recv_sem=recv_sem.at[0],
                device_id=row[0],
                device_id_type=MESH,
            ).wait_send()
    for c in outs:
        c.wait()
    assert (msgs.sends, msgs.count) == (N_SEND, N_RECV)


def exchange(*args):
    shape = jax.ShapeDtypeStruct
    anywhere = pl.BlockSpec(memory_space=pl.ANY)
    dma = pltpu.SemaphoreType.DMA
    V = pltpu.VMEM
    return pl.pallas_call(
        exchange_kernel,
        out_shape=(
            shape((NEW_DEV, R, LD), BF16),
            shape((NEW_DEV, 2, R, LD), BF16),
            shape((NEW_DEV, HALF, 2 * LK), BF16),
            shape((NEW_DEV, R, 2 * LK), BF16),
            shape((WIN, R, LD), F32),
            shape((R, 2 * LK), F32),
            shape((WIN, R, TOK), BF16),
            shape((WIN, R, KV), BF16),
        ),
        in_specs=[anywhere] * 10,
        out_specs=[anywhere] * 8,
        scratch_shapes=[
            pltpu.SMEM((LAYERS,), jnp.int32),
            pltpu.SMEM((LAYERS,), jnp.int32),
            V((WIN, SIDE, SIDE, TOK, LD), BF16),
            V((WIN, TOK, KV), BF16),
            V((OLD_DEV, R, LD), BF16),
            V((OLD_DEV, R, LD), F32),
            V((OLD_DEV, R, LD), F32),
            V((OLD_DEV, R, LK), BF16),
            V((OLD_DEV, R, LK), F32),
            V((OLD_DEV, R, LK), F32),
            V((N_SECTION, HALF, 2 * LK), BF16),
            V((N_SECTION, HALF, 2 * LK), BF16),
            V((N_SECTION, R, 2 * LK), BF16),
            V((N_SECTION, R, 2 * LK), BF16),
            V((N_SECTION, CHUNKS[0][1], LD), BF16),
            V((N_SECTION, CHUNKS[1][1], LD), BF16),
            V((N_SECTION, CHUNKS[0][1], LD), BF16),
            V((N_SECTION, CHUNKS[1][1], LD), BF16),
            V((N_SECTION, 2, R, LD), BF16),
            V((N_SECTION, 2, R, LD), BF16),
            V((WIN, N_DP, R, LD), BF16),
            V((SIDE, SIDE, R, 2 * LK), BF16),
            V((WIN, R, KV), BF16),
            V((WIN, R, TOK), BF16),
            V((WIN, R, TOK), F32),
            V((WIN, R, TOK), BF16),
            V((SIDE, SIDE, R, 2 * LK), BF16),
            V((SIDE, SIDE, R, 2 * LK), BF16),
            V((SIDE, R, 2 * LK), BF16),
            V((SIDE, R, 2 * LK), BF16),
            V((WIN, 12, R, LD), BF16),
            V((WIN, 12, R, LD), BF16),
            V((WIN, 2, HALF, LD), F32),
            V((WIN, 6, HALF, LD), BF16),
            V((WIN, 6, HALF, LD), BF16),
            V((NEW_DEV, R, LD), BF16),
            V((NEW_DEV, 2, R, LD), BF16),
            V((NEW_DEV, HALF, 2 * LK), BF16),
            V((NEW_DEV, R, 2 * LK), BF16),
            V((WIN, R, LD), F32),
            V((R, 2 * LK), F32),
            dma((N_SEND,)),
            dma((N_RECV,)),
            dma((3, WIN)),
            dma((2, 5)),
            dma((9,)),
            dma((WIN,)),
            dma((8,)),
        ],
        compiler_params=pltpu.CompilerParams(
            collective_id=0, has_side_effects=True, vmem_limit_bytes=56 * 1024 * 1024
        ),
    )(*args)


def adam(first, second, grad):
    first_new = beta_one * first + (1.0 - beta_one) * grad
    second_new = beta_two * second + (1.0 - beta_two) * grad * grad
    size = jnp.sqrt(second_new * (1.0 / corr_two)) + adam_eps
    return first_new, second_new, first_new * (1.0 / corr_one) / size


def finish_kernel(
    pa,
    pm,
    pb,
    pbm,
    ga,
    gb,
    lat,
    bw,
    out,
    new_a,
    new_b,
    fa,
    sa,
    fb,
    sb,
    step_a,
    step_b,
    pa_v,
    pm_v,
    pb_v,
    pbm_v,
    ga_v,
    gb_v,
    lat_v,
    bw_v,
    out_v,
    new_b_v,
    fa_v,
    sa_v,
    fb_v,
    sb_v,
    step_a_v,
    step_b_v,
    in_sem,
    out_sem,
):
    def copy(src, dst, sem):
        c = pltpu.make_async_copy(src, dst, sem)
        c.start()
        return c

    outs = []

    def put(src, dst):
        outs.append(copy(src, dst, out_sem.at[len(outs)]))

    ld_pm = {}
    for i, s in enumerate((2, 3, 0, 1)):
        ld_pm[s] = copy(pm.at[s], pm_v.at[s], in_sem.at[i])
    ld_ga = [copy(ga.at[w], ga_v.at[w], in_sem.at[4 + w]) for w in range(WIN)]
    ld_lat = copy(lat, lat_v, in_sem.at[6])
    ld_bw = copy(bw, bw_v, in_sem.at[7])
    ld_pb = copy(pb, pb_v, in_sem.at[8])
    ld_pbm = copy(pbm, pbm_v, in_sem.at[9])
    ld_gb = copy(gb, gb_v, in_sem.at[10])
    ld_pa = copy(pa, pa_v, in_sem.at[11])

    ld_pa.wait()
    put(pa_v, new_a)
    for s in (2, 3):
        ld_pm[s].wait()
        fa_v[s] = pm_v[s, 0].astype(F32)
        put(fa_v.at[s], fa.at[s])
        sa_v[s] = pm_v[s, 1].astype(F32)
        put(sa_v.at[s], sa.at[s])
    for w in range(WIN):
        ld_pm[w].wait()
        ld_ga[w].wait()
        f, q, d = adam(pm_v[w, 0].astype(F32), pm_v[w, 1].astype(F32), ga_v[w])
        fa_v[w] = f
        put(fa_v.at[w], fa.at[w])
        sa_v[w] = q
        put(sa_v.at[w], sa.at[w])
        step_a_v[w] = d
        put(step_a_v.at[w], step_a.at[w])
    ld_lat.wait()
    ld_bw.wait()
    for w in range(WIN):
        product = lax.dot_general(
            lat_v[w], bw_v[w], (((0,), (0,)), ((), ())), preferred_element_type=F32
        )
        out_v[w] = (adapter_scale * product).astype(BF16)
        put(out_v.at[w], out.at[w])
    ld_pb.wait()
    ld_pbm.wait()
    ld_gb.wait()
    for s in range(NEW_DEV):
        v = pb_v[s].astype(F32)
        new_b_v[s] = jnp.concatenate([v[:, :LK], v[:, LK:]], axis=0).astype(BF16)
        bm = pbm_v[s].astype(F32)
        f, q = bm[:, :LK], bm[:, LK:]
        if s < WIN:
            f, q, step_b_v[s] = adam(f, q, gb_v[:, s * LK : (s + 1) * LK])
        fb_v[s], sb_v[s] = f, q
    put(new_b_v, new_b)
    put(fb_v, fb)
    put(sb_v, sb)
    put(step_b_v, step_b)
    for c in outs:
        c.wait()


def finish(*args):
    shape = jax.ShapeDtypeStruct
    anywhere = pl.BlockSpec(memory_space=pl.ANY)
    V = pltpu.VMEM
    return pl.pallas_call(
        finish_kernel,
        out_shape=(
            shape((WIN, TOK, KV), BF16),
            shape((NEW_DEV, R, LD), BF16),
            shape((NEW_DEV, R, LK), BF16),
            shape((NEW_DEV, R, LD), F32),
            shape((NEW_DEV, R, LD), F32),
            shape((NEW_DEV, R, LK), F32),
            shape((NEW_DEV, R, LK), F32),
            shape((WIN, R, LD), F32),
            shape((WIN, R, LK), F32),
        ),
        in_specs=[anywhere] * 8,
        out_specs=[anywhere] * 9,
        scratch_shapes=[
            V((NEW_DEV, R, LD), BF16),
            V((NEW_DEV, 2, R, LD), BF16),
            V((NEW_DEV, HALF, 2 * LK), BF16),
            V((NEW_DEV, R, 2 * LK), BF16),
            V((WIN, R, LD), F32),
            V((R, 2 * LK), F32),
            V((WIN, R, TOK), BF16),
            V((WIN, R, KV), BF16),
            V((WIN, TOK, KV), BF16),
            V((NEW_DEV, R, LK), BF16),
            V((NEW_DEV, R, LD), F32),
            V((NEW_DEV, R, LD), F32),
            V((NEW_DEV, R, LK), F32),
            V((NEW_DEV, R, LK), F32),
            V((WIN, R, LD), F32),
            V((WIN, R, LK), F32),
            pltpu.SemaphoreType.DMA((12,)),
            pltpu.SemaphoreType.DMA((17,)),
        ],
        compiler_params=pltpu.CompilerParams(vmem_limit_bytes=56 * 1024 * 1024),
    )(*args)


def body(*args):
    return finish(*exchange(*args))


def solution(mesh):
    state = P("section", None, "dp")
    tokens = P("section", "dp", None)
    in_specs = (P(), P()) + (state,) * 6 + (tokens,) * 2
    out_specs = (tokens,) + (state,) * 8
    return jax.shard_map(body, mesh=mesh, in_specs=in_specs, out_specs=out_specs, check_vma=False)
```

```python
import jax
import jax.numpy as jnp
from jax import lax
from jax.experimental import pallas as pl
from jax.experimental.pallas import tpu as pltpu
from jax.sharding import PartitionSpec as P

MESH = pl.DeviceIdType.MESH
F32 = jnp.float32
BF16 = jnp.bfloat16

OLD_DEV = 3
NEW_DEV = 4
WIN = 2
LAYERS = 24
N_SECTION = 8
N_NEW = 6
N_DP = 16
SIDE = 4
R = 64
HALF = 32
CHUNKS = ((0, 16), (16, 48))
TOK = 256
LD = 1024
LK = 64
KV = 1024

adapter_scale = 2.0
beta_one = 0.9
beta_two = 0.999
adam_eps = 1e-08
corr_one = 1.0 - (0.9**10) ** 10
corr_two = 1.0 - (0.999**10) ** 10


def dot_nt(a, b):
    return lax.dot_general(a, b, (((1,), (1,)), ((), ())), preferred_element_type=F32)


def dot_nn(a, b):
    return jnp.dot(a, b, preferred_element_type=F32)


class Messages:
    def __init__(self, recv_sem):
        self.recv_sem = recv_sem
        self.count = 0

    def make(self, src, dst, device, send, receive=None):
        if receive is None:
            receive = self.recv_sem.at[self.count]
            self.count += 1
        return pltpu.make_async_remote_copy(
            src_ref=src,
            dst_ref=dst,
            send_sem=send,
            recv_sem=receive,
            device_id=device,
            device_id_type=MESH,
        )


SCHEDULE = ("F0", "F1", "own", "E1", "L0", "moments", "E2", "A0", "F2", "P2", "L1", "A1", "F3")
SCHEDULE += ("N1", "A2", "P5", "L2", "A3", "P4", "N2", "P3", "L3", "N3", "gb", "gc", "place")
N_RECV = 108


def exchange_kernel(
    old_slot_hbm,
    new_slot_hbm,
    a_old,
    a_first_old,
    a_second_old,
    b_old,
    b_first_old,
    b_second_old,
    inputs,
    cotangent,
    pa_out,
    pm_out,
    pb_out,
    pbm_out,
    ga_out,
    gb_out,
    lat_out,
    bw_out,
    old_slot,
    new_slot,
    xin,
    cot,
    av,
    mv1,
    mv2,
    bv,
    bmv1,
    bmv2,
    b_stage,
    b_recv,
    bm_stage,
    bm_recv,
    a_stage0,
    a_stage1,
    a_recv0,
    a_recv1,
    m_stage,
    m_recv,
    afull,
    bfull,
    bw,
    pulled,
    lat_acc,
    lat,
    gb_stage,
    gb_recv,
    gb_half,
    gb_last,
    gsend,
    grecv,
    hbuf,
    hsend,
    hrecv,
    pa,
    pm,
    pb,
    pbm,
    ga,
    gb,
    send_sem,
    recv_sem,
    ring_sem,
    section_sem,
    load_sem,
    x_sem,
    out_sem,
):
    me_s = lax.axis_index("section")
    me_d = lax.axis_index("dp")
    mx = me_d // SIDE
    mz = me_d % SIDE

    def at(dx, dz):
        return ((mx + dx) % SIDE) * SIDE + (mz + dz) % SIDE

    msgs = Messages(recv_sem)

    def load(src, dst, i):
        c = pltpu.make_async_copy(src, dst, load_sem.at[i])
        c.start()
        return c

    row = [(me_s, at(j, 0)) for j in range(1, SIDE)]
    column = [(me_s, at(0, j)) for j in range(1, SIDE)]
    barrier = pltpu.get_barrier_semaphore()
    for k in range(1, N_SECTION):
        pl.semaphore_signal(
            barrier, inc=1, device_id=((me_s + k) % N_SECTION, me_d), device_id_type=MESH
        )
    for device in row + column:
        pl.semaphore_signal(barrier, inc=1, device_id=device, device_id_type=MESH)

    ld_old = load(old_slot_hbm, old_slot, 7)
    ld_new = load(new_slot_hbm, new_slot, 8)
    ld_a = load(a_old, av, 1)
    ld_b = load(b_old, bv, 0)
    ld_cot = load(cotangent, cot, 2)
    ld_b1 = load(b_first_old, bmv1, 3)
    ld_b2 = load(b_second_old, bmv2, 4)
    ld_m1 = load(a_first_old, mv1, 5)
    ld_m2 = load(a_second_old, mv2, 6)

    def x_copy(w, a, b):
        ax = at(b, a) if w == 0 else at(a, b)
        return pltpu.make_async_copy(
            inputs.at[w, :, pl.ds(pl.multiple_of(ax * LD, LD), LD)],
            xin.at[w, a, b],
            x_sem.at[w],
        )

    ld_old.wait()
    ld_new.wait()
    dest = []
    for j in range(OLD_DEV):
        total = jnp.int32(0)
        for l in range(LAYERS):
            total += jnp.where(old_slot[l] == me_s * OLD_DEV + j, new_slot[l] // NEW_DEV, 0)
        dest.append(total)
    src_k, present = [], []
    for s in range(NEW_DEV):
        total, has = jnp.int32(0), jnp.int32(0)
        for l in range(LAYERS):
            hit = new_slot[l] == me_s * NEW_DEV + s
            total += jnp.where(hit, old_slot[l] // OLD_DEV, 0)
            has += jnp.where(hit, 1, 0)
        src_k.append((me_s + N_SECTION - total) % N_SECTION)
        present.append(has > 0)
    send_index = []
    for k in range(N_SECTION):
        d = (me_s + k) % N_SECTION
        pick = jnp.int32(0)
        for j in range(1, OLD_DEV):
            pick = jnp.where(dest[j] == d, j, pick)
        send_index.append(pick)

    receives = me_s < N_NEW

    def peer(k):
        return ((me_s + k) % N_SECTION, me_d)

    def sends_to(k):
        return (me_s + k) % N_SECTION < N_NEW

    def pack_b(v):
        v = v.astype(F32)
        return jnp.concatenate([v[:HALF], v[HALF:]], axis=1).astype(BF16)

    @pl.when(jnp.logical_not(receives))
    def _():
        b_recv[...] = jnp.zeros_like(b_recv)
        bm_recv[...] = jnp.zeros_like(bm_recv)
        a_recv0[...] = jnp.zeros_like(a_recv0)
        a_recv1[...] = jnp.zeros_like(a_recv1)
        m_recv[...] = jnp.zeros_like(m_recv)

    class Group:
        def __init__(self, i, stage, landing):
            self.i, self.stage, self.landing = i, stage, landing

        def message(self, k, first, size):
            return msgs.make(
                self.stage.at[pl.ds(first, size)],
                self.landing.at[pl.ds(first, size)],
                peer(k),
                section_sem.at[0, self.i],
                section_sem.at[1, self.i],
            )

    def start_all(group):
        for k in range(1, N_SECTION):
            @pl.when(sends_to(k))
            def _(k=k):
                group.message(k, k, 1).start()

    def recv_all(group):
        @pl.when(receives)
        def _():
            group.message(1, 1, N_SECTION - 1).wait_recv()

    def wait_sent(group):
        @pl.when(receives)
        def _():
            group.message(1, 1, N_NEW - 1).wait_send()

        @pl.when(jnp.logical_not(receives))
        def _():
            group.message(1, 1, N_NEW).wait_send()

    a_stage, a_recv = (a_stage0, a_stage1), (a_recv0, a_recv1)
    a_msgs = [Group(h, a_stage[h], a_recv[h]) for h in range(2)]

    def stage_a(h):
        start, size = CHUNKS[h]
        for k in range(N_SECTION):
            v = av[send_index[k], pl.ds(start, size), :]
            if k == 0:
                a_recv[h][0] = v
            else:
                a_stage[h][k] = v

    ld_a.wait()
    stage_a(0)
    ld_b.wait()
    for k in range(N_SECTION):
        v = pack_b(bv[send_index[k]])
        if k == 0:
            b_recv[0] = v
        else:
            b_stage[k] = v
    b_msgs = Group(2, b_stage, b_recv)
    pl.semaphore_wait(barrier, N_SECTION - 1 + 2 * (SIDE - 1))
    start_all(b_msgs)
    start_all(a_msgs[0])
    stage_a(1)

    for w in range(WIN):
        for b in range(SIDE):
            for a in range(SIDE):
                x_copy(w, a, b).start()

    ld_b1.wait()
    ld_b2.wait()
    ld_m1.wait()
    ld_m2.wait()
    for k in range(N_SECTION):
        bm = jnp.concatenate([bmv1[send_index[k]], bmv2[send_index[k]]], axis=1).astype(BF16)
        for i, mv in enumerate((mv1, mv2)):
            v = mv[send_index[k]].astype(BF16)
            if k == 0:
                m_recv[0, i] = v
            else:
                m_stage[k, i] = v
        if k == 0:
            bm_recv[0] = bm
        else:
            bm_stage[k] = bm
    bm_msgs = Group(3, bm_stage, bm_recv)
    m_msgs = Group(4, m_stage, m_recv)

    def nbr(w, axis, step):
        on_x = (axis == 1) == (w == 0)
        return (me_s, at(step, 0) if on_x else at(0, step))

    ag = {}
    PLUS, MINUS = 1, 3

    def ag_make(w, a, b, h, axis, step):
        na, nb = (a, b)
        if axis == 0:
            na = (a - step) % SIDE
        else:
            nb = (b - step) % SIDE
        rows = pl.ds(*CHUNKS[h])
        m = msgs.make(
            afull.at[w, a * SIDE + b, rows],
            afull.at[w, na * SIDE + nb, rows],
            nbr(w, axis, step),
            ring_sem.at[0, w],
        )
        assert (w, na, nb, h) not in ag
        ag[(w, na, nb, h)] = m
        m.start()

    def ag_on(w, a, b, h):
        if b == 0:
            if a == 0:
                ag_make(w, a, b, h, 0, 1)
                ag_make(w, a, b, h, 0, -1)
            elif a == 3 and h == 0:
                ag_make(w, a, b, h, 0, 1)
            elif a == 1 and h == 1:
                ag_make(w, a, b, h, 0, -1)
            ag_make(w, a, b, h, 1, 1)
            ag_make(w, a, b, h, 1, -1)
        elif b == 3 and h == a % 2:
            ag_make(w, a, b, h, 1, 1)
        elif b == 1 and h != a % 2:
            ag_make(w, a, b, h, 1, -1)

    def ag_own(h):
        rows = pl.ds(*CHUNKS[h])
        for s in range(NEW_DEV):
            v = a_recv[h][src_k[s]]
            v = jnp.where(present[s], v, jnp.zeros_like(v))
            pa[s, rows] = v
            if s < WIN:
                afull[s, 0, rows] = v
                ag_on(s, 0, 0, h)

    order = [(3, 0), (1, 0), (0, 3), (0, 1), (2, 0), (3, 3), (3, 1), (1, 3), (1, 1)]
    order += [(0, 2), (2, 3), (2, 1), (3, 2), (1, 2), (2, 2)]

    def ag_event(a, b, h):
        for w in range(WIN):
            ag[(w, a, b, h)].wait_recv()
            ag_on(w, a, b, h)

    recv_all(b_msgs)

    def unpack_b(v):
        v = v.astype(F32)
        return jnp.concatenate([v[:, :LK], v[:, LK:]], axis=0)

    pbs = []
    for s in range(NEW_DEV):
        v = b_recv[src_k[s]]
        v = jnp.where(present[s], v, jnp.zeros_like(v))
        pb[s] = v
        if s < WIN:
            pbs.append(unpack_b(v))
    bfull[mx, mz] = jnp.concatenate(pbs, axis=1).astype(BF16)
    bz_msgs, bx_msgs = [], []
    for device in column:
        m = msgs.make(bfull.at[mx, mz], bfull.at[mx, mz], device, send_sem.at[0])
        m.start()
        bz_msgs.append(m)


    recv_all(a_msgs[0])
    start_all(a_msgs[1])
    ag_own(0)
    for m in bz_msgs:
        m.wait_recv()
    for device in row:
        m = msgs.make(bfull.at[mx], bfull.at[mx], device, send_sem.at[1])
        m.start()
        bx_msgs.append(m)
    for a, b in order[:4]:
        ag_event(a, b, 0)

    for m in bx_msgs:
        m.wait_recv()
    for d in range(0, N_DP, 2):
        x, z = d // SIDE, d % SIDE
        lo, hi = bfull[x, z].astype(F32), bfull[x, z + 1].astype(F32)
        cols = pl.ds(d * LK, 2 * LK)
        bw[0, :, cols] = jnp.concatenate([lo[:, :LK], hi[:, :LK]], axis=1).astype(BF16)
        bw[1, :, cols] = jnp.concatenate([lo[:, LK:], hi[:, LK:]], axis=1).astype(BF16)
    ld_cot.wait()
    for w in range(WIN):
        pulled[w] = dot_nt(bw[w], cot[w]).astype(BF16)

    for w in range(WIN):
        pltpu.make_async_copy(xin.at[w], xin.at[w], x_sem.at[w]).wait()

    def partial(w, f, s):
        return dot_nn(pulled[w], xin[w, s, f])

    lat_acc[...] = jnp.zeros_like(lat_acc)

    def add_latent(w, a, b):
        lat_acc[w] += dot_nt(afull[w, a * SIDE + b], xin[w, a, b])

    def rs_nbr(w, axis, step):
        on_x = (axis == 0) == (w == 0)
        return (me_s, at(step, 0) if on_x else at(0, step))

    rs = {}

    def rs_send(key, w, i, step):
        m = msgs.make(gsend.at[w, i], grecv.at[w, i], rs_nbr(w, 0, step), ring_sem.at[1, w])
        m.start()
        rs[key] = m

    VIA = {0: 1, 1: 1, 2: -1, 3: -1}

    def rs_compute(w, s):
        gsend[w, s] = partial(w, 2, s).astype(BF16)
        gsend[w, 4 + s] = partial(w, (-VIA[s]) % SIDE, s).astype(BF16)

    def rs_start(s):
        for w in range(WIN):
            rs_send((w, "m1", s), w, s, VIA[s])
        for w in range(WIN):
            rs_send((w, "m2", s), w, 4 + s, -VIA[s])

    def rs_m3(w, s):
        f = VIA[s] % SIDE
        rs[(w, "m1", s)].wait_recv()
        gsend[w, 8 + s] = (partial(w, f, s) + grecv[w, s].astype(F32)).astype(BF16)
        rs_send((w, "m3", s), w, 8 + s, VIA[s])

    def rs_own(w, s):
        g = partial(w, 0, s)
        rs[(w, "m2", s)].wait_recv()
        rs[(w, "m3", s)].wait_recv()
        return g + grecv[w, 4 + s].astype(F32) + grecv[w, 8 + s].astype(F32)

    def rs2_send(key, w, i, step):
        m = msgs.make(hsend.at[w, i], hrecv.at[w, i], rs_nbr(w, 1, step), ring_sem.at[2, w])
        m.start()
        rs[key] = m

    top, bottom = pl.ds(0, HALF), pl.ds(HALF, HALF)

    def rs_n1(w):
        g = rs_own(w, 2)
        hsend[w, 0] = g[:HALF].astype(BF16)
        rs2_send((w, "n1", 1), w, 0, 1)
        hsend[w, 1] = g[HALF:].astype(BF16)
        rs2_send((w, "n1", 3), w, 1, -1)

    def rs_n2(w):
        g = rs_own(w, 3)
        hsend[w, 2] = g[:HALF].astype(BF16)
        rs2_send((w, "n2", 3), w, 2, -1)
        hbuf[w, 0] = g[HALF:]
        g = rs_own(w, 1)
        hsend[w, 3] = g[HALF:].astype(BF16)
        rs2_send((w, "n2", 1), w, 3, 1)
        hbuf[w, 1] = g[:HALF]

    def rs_n3(w):
        rs[(w, "n1", 1)].wait_recv()
        hsend[w, 4] = (hbuf[w, 1] + hrecv[w, 0].astype(F32)).astype(BF16)
        rs2_send((w, "n3", 1), w, 4, 1)
        rs[(w, "n1", 3)].wait_recv()
        hsend[w, 5] = (hbuf[w, 0] + hrecv[w, 1].astype(F32)).astype(BF16)
        rs2_send((w, "n3", 3), w, 5, -1)

    SUMS = (2, 3, 1, 0)
    todo = [(0, 0)]

    def latent_of_next():
        if todo:
            ta, tb = todo.pop(0)
            for w in range(WIN):
                add_latent(w, ta, tb)

    def early(blocks):
        for a, b in blocks:
            ag_event(a, b, 0)

    def late(blocks):
        for a, b in blocks:
            ag_event(a, b, 1)
            todo.append((a, b))

    def rs_first(s):
        for w in range(WIN):
            rs_compute(w, s)
        rs_start(s)

    def rs_add(s):
        for w in range(WIN):
            rs_m3(w, s)

    gx_msgs, gz_msgs, outs = [], [], []

    def gb_rows():
        while todo:
            latent_of_next()
        for w in range(WIN):
            lat[w] = lat_acc[w].astype(BF16)
        g0 = dot_nn(lat[0], cot[0]) * adapter_scale
        g1 = dot_nn(lat[1], cot[1]) * adapter_scale
        for d in range(N_DP):
            cols = slice(d * LK, (d + 1) * LK)
            g = jnp.concatenate([g0[:, cols], g1[:, cols]], axis=1).astype(BF16)
            gb_stage[d // SIDE, d % SIDE] = g
        for j in range(1, SIDE):
            m = msgs.make(
                gb_stage.at[(mx + j) % SIDE], gb_recv.at[j], row[j - 1], send_sem.at[2]
            )
            m.start()
            gx_msgs.append(m)

    def gb_columns():
        for m in gx_msgs:
            m.wait_recv()
        total = gb_stage[mx].astype(F32)
        for j in range(1, SIDE):
            total += gb_recv[j].astype(F32)
        gb_half[...] = total.astype(BF16)
        for j in range(1, SIDE):
            m = msgs.make(
                gb_half.at[(mz + j) % SIDE], gb_last.at[j], column[j - 1], send_sem.at[3]
            )
            m.start()
            gz_msgs.append(m)

    def put(src, dst, i):
        c = pltpu.make_async_copy(src, dst, out_sem.at[i])
        c.start()
        outs.append(c)

    def place_moments():
        recv_all(bm_msgs)
        recv_all(m_msgs)
        for s in range(NEW_DEV):
            v = bm_recv[src_k[s]]
            pbm[s] = jnp.where(present[s], v, jnp.zeros_like(v))
            for i in range(2):
                v = m_recv[src_k[s], i]
                pm[s, i] = jnp.where(present[s], v, jnp.zeros_like(v))
        put(pa, pa_out, 0)
        put(pb, pb_out, 1)
        put(pbm, pbm_out, 4)
        put(pm, pm_out, 5)

    def own_late():
        recv_all(a_msgs[1])
        ag_own(1)

    def send_moments():
        start_all(bm_msgs)
        start_all(m_msgs)

    def both(step):
        for w in range(WIN):
            step(w)

    steps = {
        "own": own_late,
        "moments": send_moments,
        "E1": lambda: early(order[4:9]),
        "E2": lambda: early(order[9:]),
        "L0": lambda: late(order[:4]),
        "L1": lambda: late(order[4:9]),
        "L2": lambda: late(order[9:12]),
        "L3": lambda: late(order[12:]),
        "N1": lambda: both(rs_n1),
        "N2": lambda: both(rs_n2),
        "N3": lambda: both(rs_n3),
        "gb": gb_rows,
        "gc": gb_columns,
        "place": place_moments,
    }
    for i in range(SIDE):
        steps[f"F{i}"] = lambda i=i: rs_first(SUMS[i])
        steps[f"A{i}"] = lambda i=i: rs_add(SUMS[i])
    for step in SCHEDULE:
        if step[0] == "P":
            for _ in range(int(step[1:])):
                latent_of_next()
        else:
            steps[step]()
    put(lat, lat_out, 2)
    put(bw, bw_out, 3)
    for w in range(WIN):
        ga[w] = rs_own(w, 0)
    for m in gz_msgs:
        m.wait_recv()
    total = gb_half[mz].astype(F32)
    for j in range(1, SIDE):
        total += gb_last[j].astype(F32)
    gb[...] = total
    put(gb, gb_out, 6)

    for w in range(WIN):
        rs[(w, "n2", 3)].wait_recv()
        rs[(w, "n3", 1)].wait_recv()
        ga[w, top] = adapter_scale * (
            ga[w, top] + hrecv[w, 2].astype(F32) + hrecv[w, 4].astype(F32)
        )
        rs[(w, "n2", 1)].wait_recv()
        rs[(w, "n3", 3)].wait_recv()
        ga[w, bottom] = adapter_scale * (
            ga[w, bottom] + hrecv[w, 3].astype(F32) + hrecv[w, 5].astype(F32)
        )
    put(ga, ga_out, 7)

    for group in (b_msgs, a_msgs[0], a_msgs[1], bm_msgs, m_msgs):
        wait_sent(group)
    three = pl.ds(0, SIDE - 1)
    sent = [bfull.at[0, three], bfull.at[three], gb_stage.at[three], gb_half.at[three]]
    for i, ref in enumerate(sent):
        msgs.make(ref, ref, row[0], send_sem.at[i], recv_sem.at[0]).wait_send()
    for w in range(WIN):
        for i, ref in enumerate((afull.at[w, pl.ds(0, N_DP - 1)], gsend.at[w], hsend.at[w])):
            pltpu.make_async_remote_copy(
                src_ref=ref,
                dst_ref=ref,
                send_sem=ring_sem.at[i, w],
                recv_sem=recv_sem.at[0],
                device_id=row[0],
                device_id_type=MESH,
            ).wait_send()
    for c in outs:
        c.wait()
    assert msgs.count == N_RECV


def exchange(*args):
    shape = jax.ShapeDtypeStruct
    anywhere = pl.BlockSpec(memory_space=pl.ANY)
    dma = pltpu.SemaphoreType.DMA
    V = pltpu.VMEM
    return pl.pallas_call(
        exchange_kernel,
        out_shape=(
            shape((NEW_DEV, R, LD), BF16),
            shape((NEW_DEV, 2, R, LD), BF16),
            shape((NEW_DEV, HALF, 2 * LK), BF16),
            shape((NEW_DEV, R, 2 * LK), BF16),
            shape((WIN, R, LD), F32),
            shape((R, 2 * LK), F32),
            shape((WIN, R, TOK), BF16),
            shape((WIN, R, KV), BF16),
        ),
        in_specs=[anywhere] * 10,
        out_specs=[anywhere] * 8,
        scratch_shapes=[
            pltpu.SMEM((LAYERS,), jnp.int32),
            pltpu.SMEM((LAYERS,), jnp.int32),
            V((WIN, SIDE, SIDE, TOK, LD), BF16),
            V((WIN, TOK, KV), BF16),
            V((OLD_DEV, R, LD), BF16),
            V((OLD_DEV, R, LD), F32),
            V((OLD_DEV, R, LD), F32),
            V((OLD_DEV, R, LK), BF16),
            V((OLD_DEV, R, LK), F32),
            V((OLD_DEV, R, LK), F32),
            V((N_SECTION, HALF, 2 * LK), BF16),
            V((N_SECTION, HALF, 2 * LK), BF16),
            V((N_SECTION, R, 2 * LK), BF16),
            V((N_SECTION, R, 2 * LK), BF16),
            V((N_SECTION, CHUNKS[0][1], LD), BF16),
            V((N_SECTION, CHUNKS[1][1], LD), BF16),
            V((N_SECTION, CHUNKS[0][1], LD), BF16),
            V((N_SECTION, CHUNKS[1][1], LD), BF16),
            V((N_SECTION, 2, R, LD), BF16),
            V((N_SECTION, 2, R, LD), BF16),
            V((WIN, N_DP, R, LD), BF16),
            V((SIDE, SIDE, R, 2 * LK), BF16),
            V((WIN, R, KV), BF16),
            V((WIN, R, TOK), BF16),
            V((WIN, R, TOK), F32),
            V((WIN, R, TOK), BF16),
            V((SIDE, SIDE, R, 2 * LK), BF16),
            V((SIDE, SIDE, R, 2 * LK), BF16),
            V((SIDE, R, 2 * LK), BF16),
            V((SIDE, R, 2 * LK), BF16),
            V((WIN, 12, R, LD), BF16),
            V((WIN, 12, R, LD), BF16),
            V((WIN, 2, HALF, LD), F32),
            V((WIN, 6, HALF, LD), BF16),
            V((WIN, 6, HALF, LD), BF16),
            V((NEW_DEV, R, LD), BF16),
            V((NEW_DEV, 2, R, LD), BF16),
            V((NEW_DEV, HALF, 2 * LK), BF16),
            V((NEW_DEV, R, 2 * LK), BF16),
            V((WIN, R, LD), F32),
            V((R, 2 * LK), F32),
            dma((4,)),
            dma((N_RECV,)),
            dma((3, WIN)),
            dma((2, 5)),
            dma((9,)),
            dma((WIN,)),
            dma((8,)),
        ],
        compiler_params=pltpu.CompilerParams(
            collective_id=0, has_side_effects=True, vmem_limit_bytes=56 * 1024 * 1024
        ),
    )(*args)


def adam(first, second, grad):
    first_new = beta_one * first + (1.0 - beta_one) * grad
    second_new = beta_two * second + (1.0 - beta_two) * grad * grad
    size = jnp.sqrt(second_new * (1.0 / corr_two)) + adam_eps
    return first_new, second_new, first_new * (1.0 / corr_one) / size


def finish_kernel(
    pa,
    pm,
    pb,
    pbm,
    ga,
    gb,
    lat,
    bw,
    out,
    new_a,
    new_b,
    fa,
    sa,
    fb,
    sb,
    step_a,
    step_b,
    pa_v,
    pm_v,
    pb_v,
    pbm_v,
    ga_v,
    gb_v,
    lat_v,
    bw_v,
    out_v,
    new_b_v,
    fa_v,
    sa_v,
    fb_v,
    sb_v,
    step_a_v,
    step_b_v,
    in_sem,
    out_sem,
):
    def copy(src, dst, sem):
        c = pltpu.make_async_copy(src, dst, sem)
        c.start()
        return c

    outs = []

    def put(src, dst):
        outs.append(copy(src, dst, out_sem.at[len(outs)]))

    ld_pm = {}
    for i, s in enumerate((2, 3, 0, 1)):
        ld_pm[s] = copy(pm.at[s], pm_v.at[s], in_sem.at[i])
    ld_ga = [copy(ga.at[w], ga_v.at[w], in_sem.at[4 + w]) for w in range(WIN)]
    ld_lat = copy(lat, lat_v, in_sem.at[6])
    ld_bw = copy(bw, bw_v, in_sem.at[7])
    ld_pb = copy(pb, pb_v, in_sem.at[8])
    ld_pbm = copy(pbm, pbm_v, in_sem.at[9])
    ld_gb = copy(gb, gb_v, in_sem.at[10])
    ld_pa = copy(pa, pa_v, in_sem.at[11])

    ld_pa.wait()
    put(pa_v, new_a)
    for s in (2, 3):
        ld_pm[s].wait()
        fa_v[s] = pm_v[s, 0].astype(F32)
        put(fa_v.at[s], fa.at[s])
        sa_v[s] = pm_v[s, 1].astype(F32)
        put(sa_v.at[s], sa.at[s])
    for w in range(WIN):
        ld_pm[w].wait()
        ld_ga[w].wait()
        f, q, d = adam(pm_v[w, 0].astype(F32), pm_v[w, 1].astype(F32), ga_v[w])
        fa_v[w] = f
        put(fa_v.at[w], fa.at[w])
        sa_v[w] = q
        put(sa_v.at[w], sa.at[w])
        step_a_v[w] = d
        put(step_a_v.at[w], step_a.at[w])
    ld_lat.wait()
    ld_bw.wait()
    for w in range(WIN):
        product = lax.dot_general(
            lat_v[w], bw_v[w], (((0,), (0,)), ((), ())), preferred_element_type=F32
        )
        out_v[w] = (adapter_scale * product).astype(BF16)
        put(out_v.at[w], out.at[w])
    ld_pb.wait()
    ld_pbm.wait()
    ld_gb.wait()
    for s in range(NEW_DEV):
        v = pb_v[s].astype(F32)
        new_b_v[s] = jnp.concatenate([v[:, :LK], v[:, LK:]], axis=0).astype(BF16)
        bm = pbm_v[s].astype(F32)
        f, q = bm[:, :LK], bm[:, LK:]
        if s < WIN:
            f, q, step_b_v[s] = adam(f, q, gb_v[:, s * LK : (s + 1) * LK])
        fb_v[s], sb_v[s] = f, q
    put(new_b_v, new_b)
    put(fb_v, fb)
    put(sb_v, sb)
    put(step_b_v, step_b)
    for c in outs:
        c.wait()


def finish(*args):
    shape = jax.ShapeDtypeStruct
    anywhere = pl.BlockSpec(memory_space=pl.ANY)
    V = pltpu.VMEM
    return pl.pallas_call(
        finish_kernel,
        out_shape=(
            shape((WIN, TOK, KV), BF16),
            shape((NEW_DEV, R, LD), BF16),
            shape((NEW_DEV, R, LK), BF16),
            shape((NEW_DEV, R, LD), F32),
            shape((NEW_DEV, R, LD), F32),
            shape((NEW_DEV, R, LK), F32),
            shape((NEW_DEV, R, LK), F32),
            shape((WIN, R, LD), F32),
            shape((WIN, R, LK), F32),
        ),
        in_specs=[anywhere] * 8,
        out_specs=[anywhere] * 9,
        scratch_shapes=[
            V((NEW_DEV, R, LD), BF16),
            V((NEW_DEV, 2, R, LD), BF16),
            V((NEW_DEV, HALF, 2 * LK), BF16),
            V((NEW_DEV, R, 2 * LK), BF16),
            V((WIN, R, LD), F32),
            V((R, 2 * LK), F32),
            V((WIN, R, TOK), BF16),
            V((WIN, R, KV), BF16),
            V((WIN, TOK, KV), BF16),
            V((NEW_DEV, R, LK), BF16),
            V((NEW_DEV, R, LD), F32),
            V((NEW_DEV, R, LD), F32),
            V((NEW_DEV, R, LK), F32),
            V((NEW_DEV, R, LK), F32),
            V((WIN, R, LD), F32),
            V((WIN, R, LK), F32),
            pltpu.SemaphoreType.DMA((12,)),
            pltpu.SemaphoreType.DMA((17,)),
        ],
        compiler_params=pltpu.CompilerParams(vmem_limit_bytes=56 * 1024 * 1024),
    )(*args)


def body(*args):
    return finish(*exchange(*args))


def solution(mesh):
    state = P("section", None, "dp")
    tokens = P("section", "dp", None)
    in_specs = (P(), P()) + (state,) * 6 + (tokens,) * 2
    out_specs = (tokens,) + (state,) * 8
    return jax.shard_map(body, mesh=mesh, in_specs=in_specs, out_specs=out_specs, check_vma=False)
```
